32 devices in a mesh: dp: 4 (over x, core), latent: 8 (over z, y).
Axes of the slice: x: 2, y: 2, z: 4, core: 2. Of those that a mesh axis runs over, the one named last changes fastest.
Arguments:
- activations: bfloat16 [4096, 8192], P(('dp', 'latent')), may hold values from -6 to 6
- owner_ids: int32 [4096, 2], P(('dp', 'latent')), may hold values from 0 to 7, all different within a row; in each aligned block of 128 rows (0 to 127, 128 to 255, ...) at most 34 rows name the same one
- block_mask: int32 [4096, 2, 8], P(('dp', 'latent')), may hold values 0 or 1
- latent_codes: bfloat16 [4096, 2, 1024], P(('dp', 'latent')), may hold values from 0.099609375 to 4
- w_dec: bfloat16 [8192, 8192], P('latent', 'dp'), may hold values from -0.125 to 0.125
- b_dec: float32 [8192], replicated, may hold values from -3 to 3
Outputs:
- rebuilt: bfloat16 [4096, 8192], P(('dp', 'latent'))
- decoder_grad: bfloat16 [8192, 8192], P('latent', 'dp')
The draws below stay inside these ranges and needn't reach their ends.
Inputs may be any that keep to these rules, and one draw needn't show every extreme that they name: `owner_ids`: each row names 2 different owners; among the rows of one device no owner is named more than 34 times, and in every draw some device names some owner exactly 34 times.
All inputs are finite; a program needn't handle non-finite values. No bound on the sum of `block_mask` on one device may be relied on, other than what follows from the above.
Results may differ from the reference program's by a relative error of at most 0.0047.
Values may be sent and summed in bfloat16 or wider, within the bound.
No kernel may reach another device: no remote copies, remote signals or barrier semaphores. Data moves between devices by JAX's collectives and lax.ppermute only.
A program may use at most 128 MiB of HBM per device.

```python
import math
import jax
import jax.numpy as jnp
import numpy as np
from jax import lax

D = 8192
BLK = 128
BPO = 8
G = 2
R_DEV = 128
SLAB = 1024
ROWS = 4096
LATENTS = 8192
MOST = 34
N_DP = 4
N_LATENT = 8


def plant(drawn, rng, low, largest):
    shape = drawn.shape
    index_at = [jax.random.randint(jax.random.fold_in(rng, axis), (), 0, shape[axis]) for axis in range(len(shape))]
    drawn = drawn.at[tuple(index_at)].set(low)
    longest = shape.index(max(shape))
    index_at[longest] = (index_at[longest] + 1) % shape[longest]
    return drawn.at[tuple(index_at)].set(largest)


def block_scale(rng, extent, split, smallest, high):
    factor_of = 1.0
    for dim, parts in split:
        heights = jax.random.uniform(jax.random.fold_in(jax.random.fold_in(rng, 6), dim), (parts,), jnp.float32, smallest / len(split), high / len(split))
        factor_of = factor_of * jnp.repeat(jnp.exp(heights), extent[dim] // parts).reshape((-1,) + (1,) * (len(extent) - 1 - dim))
    return factor_of


def shared_out(own_key, own, number, rows, number_of, top, most, skew):
    order = jax.random.permutation(own_key, number_of)
    packed, ordinary = portions_of(number_of, rows * top, most, skew, True), portions_of(number_of, rows * top, most, skew, False)
    places = jnp.arange(number_of)

    def named(lengths, rotation):
        used = int((lengths > 0).sum())
        fixed = max(1, used // 4)
        moved = fixed + (places - fixed + rotation * (used - fixed)) % max(1, number_of - fixed)
        return jnp.zeros((number_of,), jnp.int32).at[order[jnp.where(places < fixed, places, moved)]].set(jnp.asarray(lengths, jnp.int32))

    lengths = jnp.where(number % 4 == 0, named(packed, number // 4), named(ordinary, number - number // 4 - 1))
    mixed = jax.random.permutation(jax.random.fold_in(own, 3), number_of)
    donor, taker = mixed[0:number_of // 2 * 2:2], mixed[1:number_of // 2 * 2:2]
    room = jnp.minimum(lengths[donor] - 1, most - lengths[taker]) // 2
    room = jnp.where((donor == order[0]) | (taker == order[0]) | (lengths[taker] == 0), 0, jnp.maximum(room, 0))
    moved = jax.random.randint(jax.random.fold_in(own, 4), (number_of // 2,), 0, 1 << 20) % (room + 1)
    lengths = lengths.at[donor].add(-moved).at[taker].add(moved)
    labels = jnp.searchsorted(jnp.cumsum(lengths), jnp.arange(rows * top), side="right").astype(jnp.int32)
    grid = labels.reshape(top, rows).T
    grid = grid[jax.random.permutation(jax.random.fold_in(own, 1), rows)]
    rotation = jax.random.randint(jax.random.fold_in(own, 2), (rows, 1), 0, top)
    return jnp.take_along_axis(grid, (jnp.arange(top)[None, :] + rotation) % top, axis=1)


def portions_of(count, total, limit, slope, full):
    weights = [(1 << 20) // math.isqrt(rank ** slope) + 1 for rank in range(1, count + 1)]
    largest = limit if full else min(limit, max(-(-total // count), total * weights[0] // sum(weights)))
    least = 1 if total - largest >= count - 1 else 0
    counts, spare = [largest] + [least] * (count - 1), total - largest - least * (count - 1)
    while spare > 0:
        candidates = [i for i in range(1, count) if counts[i] < largest] or [i for i in range(1, count) if counts[i] < limit]
        mass, budget = sum([weights[i] for i in candidates]), spare
        for i in candidates:
            more = min(limit - counts[i], max(1, budget * weights[i] // mass), spare)
            counts[i] = counts[i] + more
            spare = spare - more
    return np.array(counts)


def scatter_about(key, dims, deviation, bound, pieces=(), kind=jnp.bfloat16):
    drawn = deviation * jax.random.normal(key, dims, jnp.float32)
    if pieces:
        drawn = drawn * block_scale(key, dims, pieces, -0.22, 0.18)
    return jnp.clip(drawn, -bound, bound).astype(kind)


def setup_inputs(seed: int = 0) -> dict:
    key_list = jax.random.split(jax.random.key(seed), 7)
    activations = scatter_about(key_list[0], (ROWS, D), 1.0, 6.0, ((0, 32),))
    owner_ids_keys = jax.random.split(jax.random.fold_in(key_list[1], 1), ROWS // R_DEV)
    owner_ids_turns = jax.random.permutation(jax.random.fold_in(key_list[1], 3), ROWS // R_DEV)
    owner_ids = jax.vmap(lambda own, number: shared_out(jax.random.fold_in(key_list[1], 2), own, number, R_DEV, N_LATENT, G, MOST, 2))(owner_ids_keys, owner_ids_turns).reshape((ROWS, G))
    block_mask = plant((jax.random.randint(key_list[2], (ROWS, G, BPO), 0, 2) < 1).astype(jnp.int32), jax.random.fold_in(key_list[2], 1), 0, 1)
    latent_codes = jnp.clip(jnp.exp(math.log(4.0) - 3.6927934 * jax.random.uniform(key_list[3], (ROWS, G, SLAB), jnp.float32) ** block_scale(key_list[3], (ROWS, G, SLAB), ((0, 32),), -0.2, 0.2)), 0.099609375, 4.0).astype(jnp.bfloat16)
    w_dec = scatter_about(key_list[4], (LATENTS, D), (G * SLAB) ** -0.5, 0.125, ((0, 8), (1, 4)))
    b_dec = scatter_about(key_list[5], (D,), 0.5, 3.0, (), jnp.float32)
    return {"activations": activations, "owner_ids": owner_ids, "block_mask": block_mask, "latent_codes": latent_codes, "w_dec": w_dec, "b_dec": b_dec}


loss_scale = 1.0 / 32.0


def reference(activations, owner_ids, block_mask, latent_codes, w_dec, b_dec):
    slab = BPO * BLK
    visit_count = ROWS * G
    capacity = N_DP * N_LATENT * MOST
    flat_owner = owner_ids.reshape(-1)
    live = block_mask.astype(latent_codes.dtype)[:, :, :, None]
    used = (latent_codes.reshape(ROWS, G, BPO, BLK) * live).reshape(visit_count, slab)
    panels = w_dec.reshape(N_LATENT, slab, D)

    def select(owner):
        hits = flat_owner == owner
        total = jnp.sum(hits.astype(jnp.int32))
        places = jnp.nonzero(hits, size=capacity, fill_value=0)[0].astype(jnp.int32)
        filled = jnp.arange(capacity) < total
        values = jnp.where(filled[:, None], used[places], jnp.zeros((), used.dtype))
        return places // G, values

    def forward(running, owner):
        row_ids, values = select(owner)
        contribution = jnp.dot(values, panels[owner], preferred_element_type=jnp.float32).astype(jnp.bfloat16)
        return running.at[row_ids].add(contribution.astype(jnp.float32)), None

    start_sum = jnp.zeros((ROWS, D), jnp.float32) + b_dec[None, :].astype(jnp.float32)
    rebuilt_wide, _ = lax.scan(forward, start_sum, jnp.arange(N_LATENT))
    rebuilt = rebuilt_wide.astype(jnp.bfloat16)
    errors = (rebuilt_wide - activations.astype(jnp.float32)).astype(jnp.bfloat16)

    def backward(owner):
        row_ids, values = select(owner)
        summed = jnp.dot(values.T, errors[row_ids], preferred_element_type=jnp.float32) * loss_scale
        return summed.astype(jnp.bfloat16)

    gradient = lax.map(backward, jnp.arange(N_LATENT)).reshape(LATENTS, D)
    return rebuilt, gradient
```

```python
import functools

import jax
import jax.numpy as jnp
from jax import lax
from jax.experimental import pallas as pl
from jax.experimental.pallas import tpu as pltpu
from jax.sharding import PartitionSpec as P

loss_scale = 1.0 / 32.0
SPARE = 2
STACK = 8
F32 = jnp.float32
BF16 = jnp.bfloat16


def mm(a, b):
    return jnp.dot(a, b, preferred_element_type=F32)


def swap_matrix(outer, inner):
    size = outer * inner * SPARE
    to = lax.broadcasted_iota(jnp.int32, (size, size), 0)
    at = lax.broadcasted_iota(jnp.int32, (size, size), 1)
    to_inner, to_outer = to // (outer * SPARE), to % (outer * SPARE) // SPARE
    at_outer, at_inner = at // (inner * SPARE), at % (inner * SPARE) // SPARE
    same = (to_inner == at_inner) & (to_outer == at_outer) & (to % SPARE == at % SPARE)
    return same.astype(F32).astype(BF16)


def pack_kernel(me_ref, owner_ref, mask_ref, codes_ref, *outs):
    messages, (pick_ref, pick_spare_ref, place_ref, place_spare_ref) = outs[:-4], outs[-4:]
    owners = len(messages)
    rows, visits = owner_ref.shape
    width = codes_ref.shape[1] // visits
    blocks = mask_ref.shape[1] // visits
    block = width // blocks
    main = rows * visits // owners
    slots = owners * (main + SPARE)
    relative = owner_ref[...] ^ me_ref[0]
    eye = lax.broadcasted_iota(jnp.int32, (rows, rows), 0) == lax.broadcasted_iota(jnp.int32, (rows, rows), 1)
    columns = [relative[:, g : g + 1] for g in range(visits)]
    lanes = [jnp.sum(jnp.where(eye, column, 0), axis=0, keepdims=True) for column in columns]
    column, lane = jnp.concatenate(columns, axis=0), jnp.concatenate(lanes, axis=1)
    total = rows * visits
    down = lax.broadcasted_iota(jnp.int32, (total, total), 0)
    across = lax.broadcasted_iota(jnp.int32, (total, total), 1)
    same = column == lane

    def slot_of(owner, place):
        return jnp.where(place < main, owner * main + place, owners * main + owner * SPARE + place - main)

    slot_lane = slot_of(lane, jnp.sum(jnp.where(same & (down < across), 1, 0), axis=0, keepdims=True))
    slot_column = slot_of(column, jnp.sum(jnp.where(same & (across < down), 1, 0), axis=1, keepdims=True))
    place = (lax.broadcasted_iota(jnp.int32, (slots, total), 0) == slot_lane).astype(F32)
    pick = (lax.broadcasted_iota(jnp.int32, (total, slots), 1) == slot_column).astype(F32)
    place_rows = sum(place[:, g * rows : (g + 1) * rows] for g in range(visits)).astype(BF16)
    pick_rows = sum(pick[g * rows : (g + 1) * rows, :] for g in range(visits)).astype(BF16)
    pick_ref[...] = pick_rows[:, : owners * main]
    pick_spare_ref[...] = pick_rows[:, owners * main :]
    place_ref[...] = place_rows[: owners * main, :]
    place_spare_ref[...] = place_rows[owners * main :, :]
    used = jnp.concatenate(
        [
            jnp.concatenate(
                [
                    codes_ref[:, g * width + b * block : g * width + (b + 1) * block]
                    * mask_ref[:, g * blocks + b : g * blocks + b + 1].astype(F32).astype(BF16)
                    for b in range(blocks)
                ],
                axis=1,
            )
            for g in range(visits)
        ],
        axis=0,
    )
    sorted_codes = mm(place.astype(BF16), used).astype(BF16)
    part = width // STACK
    for k in range(owners):
        for q in range(STACK):
            messages[k][q * main : (q + 1) * main, :] = sorted_codes[
                k * main : (k + 1) * main, q * part : (q + 1) * part
            ]
    spare = jnp.concatenate(
        [sorted_codes[owners * main :, q * part : (q + 1) * part] for q in range(STACK)], axis=0
    )
    spare = mm(swap_matrix(STACK, owners), spare).astype(BF16)
    for k in range(owners):
        messages[k][STACK * main :, :] = spare[k * STACK * SPARE : (k + 1) * STACK * SPARE, :]


def unpack_kernel(*refs):
    messages, out_ref = refs[:-1], refs[-1]
    owners = len(messages)
    main = messages[0].shape[0] // STACK - SPARE
    part = messages[0].shape[1]
    for q in range(STACK):
        for k in range(owners):
            out_ref[k * main : (k + 1) * main, q * part : (q + 1) * part] = messages[k][
                q * main : (q + 1) * main, :
            ]
    spare = jnp.concatenate([message[STACK * main :, :] for message in messages], axis=0)
    spare = mm(swap_matrix(owners, STACK), spare).astype(BF16)
    for q in range(STACK):
        out_ref[owners * main :, q * part : (q + 1) * part] = spare[
            q * owners * SPARE : (q + 1) * owners * SPARE, :
        ]


def decode_kernel(codes_ref, w_ref, *rest):
    messages, spare_ref = rest[:-1], rest[-1]
    owners = len(messages)
    main = messages[0].shape[0] // STACK - SPARE
    q = pl.program_id(0)
    term = mm(codes_ref[...], w_ref[...]).astype(BF16)
    at = pl.multiple_of(q * main, main)
    for k in range(owners):
        messages[k][pl.ds(at, main), :] = term[k * main : (k + 1) * main, :]
    spare_ref[pl.ds(pl.multiple_of(q * owners * SPARE, owners * SPARE), owners * SPARE), :] = term[
        owners * main :, :
    ]

    @pl.when(q == STACK - 1)
    def _():
        spare = mm(swap_matrix(STACK, owners), spare_ref[...]).astype(BF16)
        for k in range(owners):
            messages[k][STACK * main :, :] = spare[k * STACK * SPARE : (k + 1) * STACK * SPARE, :]


def combine_kernel(owners, place_in_ref, pick_ref, pick_spare_ref, place_ref, place_spare_ref, b_ref, act_ref, *rest):
    terms, rest = rest[:owners], rest[owners:]
    rebuilt_ref, messages, (spare_in_ref, spare_out_ref) = rest[-3 - owners], rest[-2 - owners : -2], rest[-2:]
    main = terms[0].shape[0] // STACK - SPARE
    q = pl.program_id(0)

    @pl.when(q == 0)
    def _():
        spare = jnp.concatenate([term[STACK * main :, :] for term in terms], axis=0)
        spare_in_ref[...] = mm(swap_matrix(owners, STACK), spare).astype(BF16)

    at = pl.multiple_of(q * main, main)
    spare_at = pl.ds(pl.multiple_of(q * owners * SPARE, owners * SPARE), owners * SPARE)
    arrived = jnp.concatenate([term[pl.ds(at, main), :] for term in terms], axis=0)
    wide = b_ref[...] + (mm(pick_ref[...], arrived) + mm(pick_spare_ref[...], spare_in_ref[spare_at, :]))
    rebuilt_ref[...] = wide.astype(BF16)
    errors = (wide - act_ref[...].astype(F32)).astype(BF16)
    placed = mm(place_ref[...], errors).astype(BF16)
    for k in range(owners):
        messages[k][pl.ds(at, main), :] = placed[k * main : (k + 1) * main, :]
    spare_out_ref[spare_at, :] = mm(place_spare_ref[...], errors).astype(BF16)

    @pl.when(q == STACK - 1)
    def _():
        spare = mm(swap_matrix(STACK, owners), spare_out_ref[...]).astype(BF16)
        for k in range(owners):
            messages[k][STACK * main :, :] = spare[k * STACK * SPARE : (k + 1) * STACK * SPARE, :]


def turn_kernel(groups, *refs):
    codes, outs, spare_ref = refs[:groups], refs[groups : 2 * groups], refs[2 * groups]
    for j in range(groups):
        main = outs[j].shape[1]
        outs[j][...] = codes[j][:main, :].astype(F32).T.astype(BF16)
    spare = jnp.concatenate([code[outs[0].shape[1] :, :] for code in codes], axis=0)
    spare_ref[...] = spare.astype(F32).T.astype(BF16)


def gradient_kernel(groups, owners, *refs):
    codes, spare_codes_ref = refs[:groups], refs[groups]
    messages = refs[groups + 1 : groups + 1 + groups * owners]
    out_ref, spare_ref = refs[-2:]
    main = messages[0].shape[0] // STACK - SPARE
    q = pl.program_id(0)

    @pl.when(q == 0)
    def _():
        swap = swap_matrix(owners, STACK)
        for j in range(groups):
            spare = jnp.concatenate([m[STACK * main :, :] for m in messages[j * owners : (j + 1) * owners]], axis=0)
            spare_ref[j] = mm(swap, spare).astype(BF16)

    at = pl.multiple_of(q * main, main)
    spare_at = pl.ds(pl.multiple_of(q * owners * SPARE, owners * SPARE), owners * SPARE)
    total = mm(spare_codes_ref[...], jnp.concatenate([spare_ref[j, spare_at, :] for j in range(groups)], axis=0))
    for j in range(groups):
        arrived = jnp.concatenate([m[pl.ds(at, main), :] for m in messages[j * owners : (j + 1) * owners]], axis=0)
        total += mm(codes[j][...], arrived)
    out_ref[...] = (total * loss_scale).astype(BF16)


def whole(shape):
    return pl.BlockSpec(shape, lambda *_: (0,) * len(shape))


def params(mib):
    return pltpu.CompilerParams(vmem_limit_bytes=mib * 2**20)


def cost(flops, moved):
    return pl.CostEstimate(flops=int(flops), bytes_accessed=int(moved), transcendentals=0)


def on_device(activations, owner_ids, block_mask, latent_codes, w_dec, b_dec):
    rows, visits = owner_ids.shape
    width = latent_codes.shape[2]
    model = activations.shape[1]
    owners, groups = lax.axis_size("latent"), lax.axis_size("dp")
    main = rows * visits // owners
    slots = owners * (main + SPARE)
    depth = STACK * (main + SPARE)
    local = w_dec.shape[1]
    part = local // STACK
    me, group = lax.axis_index("latent"), lax.axis_index("dp")

    def move(x, j, k):
        if j == 0 and k == 0:
            return x
        pairs = [(i, i ^ (j * owners + k)) for i in range(groups * owners)]
        return lax.ppermute(x, ("dp", "latent"), pairs)

    far_first = list(range(owners - 1, -1, -1))

    packed = pl.pallas_call(
        pack_kernel,
        grid_spec=pltpu.PrefetchScalarGridSpec(
            num_scalar_prefetch=1,
            grid=(1,),
            in_specs=[whole((rows, visits)), whole((rows, visits * block_mask.shape[2])), whole((rows, visits * width))],
            out_specs=[whole((depth, width // STACK))] * owners
            + [whole((rows, owners * main)), whole((rows, owners * SPARE))]
            + [whole((owners * main, rows)), whole((owners * SPARE, rows))],
        ),
        out_shape=[jax.ShapeDtypeStruct((depth, width // STACK), BF16)] * owners
        + [
            jax.ShapeDtypeStruct(s, BF16)
            for s in [(rows, owners * main), (rows, owners * SPARE), (owners * main, rows), (owners * SPARE, rows)]
        ],
        compiler_params=params(16),
        cost_estimate=cost(2 * slots * rows * visits * width, 4 * rows * visits * width),
        name="pack",
    )(
        me.reshape(1),
        owner_ids,
        block_mask.reshape(rows, -1),
        latent_codes.reshape(rows, -1),
    )
    outgoing, picks = packed[:owners], packed[owners:]
    arrived = [None] * owners
    for k in far_first:
        arrived[k] = move(outgoing[k], 0, k)
    codes = [None] * groups
    codes[0] = pl.pallas_call(
        unpack_kernel,
        out_shape=jax.ShapeDtypeStruct((slots, width), BF16),
        compiler_params=params(8),
        cost_estimate=cost(0, 4 * slots * width),
        name="unpack",
    )(*arrived)
    for j in range(1, groups):
        low = j & -j
        codes[j] = move(codes[j ^ low], low, 0) if j != low else move(codes[0], j, 0)

    decode = pl.pallas_call(
        decode_kernel,
        grid=(STACK,),
        in_specs=[whole((slots, width)), pl.BlockSpec((width, part), lambda q: (0, q))],
        out_specs=[whole((depth, part))] * owners,
        out_shape=[jax.ShapeDtypeStruct((depth, part), BF16)] * owners,
        scratch_shapes=[pltpu.VMEM((STACK * owners * SPARE, part), BF16)],
        compiler_params=params(16),
        cost_estimate=cost(2 * slots * width * local, 2 * (width * local + slots * (width + local))),
        name="decode",
    )
    terms = [None] * groups
    for j in range(groups):
        decoded = decode(codes[j], w_dec)
        terms[j] = [None] * owners
        for k in far_first:
            terms[j][k] = move(decoded[k], j, k)

    rebuilt, errors = None, [None] * groups
    for j in range(groups):
        first = rebuilt is None
        outs = pl.pallas_call(
            functools.partial(combine_kernel, owners),
            grid_spec=pltpu.PrefetchScalarGridSpec(
                num_scalar_prefetch=1,
                grid=(STACK,),
                in_specs=[whole(p.shape) for p in picks]
                + [
                    pl.BlockSpec((1, part), lambda q, at: (0, at[0] * STACK + q)),
                    pl.BlockSpec((rows, part), lambda q, at: (0, at[0] * STACK + q)),
                ]
                + [whole((depth, part))] * owners
                + ([] if first else [pl.BlockSpec(memory_space=pl.ANY)]),
                out_specs=[pl.BlockSpec((rows, part), lambda q, at: (0, at[0] * STACK + q))]
                + [whole((depth, part))] * owners,
                scratch_shapes=[pltpu.VMEM((STACK * owners * SPARE, part), BF16)] * 2,
            ),
            out_shape=[jax.ShapeDtypeStruct((rows, model), BF16)]
            + [jax.ShapeDtypeStruct((depth, part), BF16)] * owners,
            input_output_aliases={} if first else {7 + owners: 0},
            compiler_params=params(16),
            cost_estimate=cost(4 * slots * rows * local, 2 * local * (2 * slots + 2 * rows)),
            name="combine",
        )((group ^ j).reshape(1), *picks, b_dec.reshape(1, -1), activations, *terms[j], *([] if first else [rebuilt]))
        rebuilt = outs[0]
        errors[j] = [None] * owners
        for k in far_first:
            errors[j][k] = move(outs[1 + k], j, k)

    turned = pl.pallas_call(
        functools.partial(turn_kernel, groups),
        out_shape=[jax.ShapeDtypeStruct((width, owners * main), BF16)] * groups
        + [jax.ShapeDtypeStruct((width, groups * owners * SPARE), BF16)],
        compiler_params=params(24),
        cost_estimate=cost(0, 4 * groups * slots * width),
        name="turn",
    )(*codes)
    gradient = pl.pallas_call(
        functools.partial(gradient_kernel, groups, owners),
        grid=(STACK,),
        in_specs=[whole(t.shape) for t in turned] + [whole((depth, part))] * (groups * owners),
        out_specs=pl.BlockSpec((width, part), lambda q: (0, q)),
        out_shape=jax.ShapeDtypeStruct((width, local), BF16),
        scratch_shapes=[pltpu.VMEM((groups, STACK * owners * SPARE, part), BF16)],
        compiler_params=params(32),
        cost_estimate=cost(2 * groups * slots * width * local, 2 * (width * local + groups * slots * (width + local))),
        name="gradient",
    )(*turned, *[m for j in range(groups) for m in errors[j]])
    return rebuilt, gradient


def on_device_wide(activations, owner_ids, block_mask, latent_codes, w_dec, b_dec):
    row_count, visit_count = owner_ids.shape
    block_count = block_mask.shape[2]
    slab_width = latent_codes.shape[2]
    block_width = slab_width // block_count
    model_width = activations.shape[1]
    owners = lax.axis_size("latent")
    groups = lax.axis_size("dp")
    capacity = row_count * visit_count // owners + SPARE
    live = block_mask.astype(latent_codes.dtype)[:, :, :, None]
    used = (latent_codes.reshape(row_count, visit_count, block_count, block_width) * live).reshape(-1, slab_width)
    onehot = (owner_ids[:, :, None] == lax.broadcasted_iota(jnp.int32, (1, 1, owners), 2)).astype(jnp.int32)
    per_row = jnp.sum(onehot, axis=1)
    before = jnp.cumsum(per_row, axis=0) - per_row
    position = jnp.sum(onehot * before[:, None, :], axis=2)
    target_slot = (owner_ids * capacity + position).reshape(-1)
    outgoing = jnp.zeros((owners * capacity, slab_width), latent_codes.dtype)
    outgoing = outgoing.at[target_slot].set(used).reshape(owners, capacity, slab_width)
    arrived = lax.all_to_all(outgoing, "latent", split_axis=0, concat_axis=0, tiled=True)
    copies = lax.all_gather(arrived, "dp", axis=0, tiled=True)
    decoded = mm(copies.reshape(-1, slab_width), w_dec).astype(BF16)
    local = w_dec.shape[1]
    returned = lax.all_to_all(
        decoded.reshape(groups * owners, capacity, local), ("dp", "latent"), split_axis=0, concat_axis=0, tiled=True
    )
    returned = returned.reshape(groups, owners * capacity, local)
    gathered = returned[:, target_slot].reshape(groups, row_count, visit_count, local)
    gathered = jnp.sum(gathered, axis=2, dtype=F32).transpose(1, 0, 2).reshape(row_count, model_width)
    rebuilt_wide = b_dec[None, :] + gathered
    errors = (rebuilt_wide - activations.astype(F32)).astype(BF16)
    parts = jnp.repeat(errors.reshape(row_count, groups, local).transpose(1, 0, 2), visit_count, axis=1)
    error_slots = jnp.zeros((groups, owners * capacity, local), BF16).at[:, target_slot].set(parts)
    error_parts = lax.all_to_all(
        error_slots.reshape(groups * owners, capacity, local), ("dp", "latent"), split_axis=0, concat_axis=0, tiled=True
    )
    gradient = jnp.einsum("nsi,nsd->id", copies, error_parts, preferred_element_type=F32) * loss_scale
    return rebuilt_wide.astype(BF16), gradient.astype(BF16)


def solution(mesh):
    placed = (
        P(("dp", "latent"), None),
        P(("dp", "latent"), None),
        P(("dp", "latent"), None, None),
        P(("dp", "latent"), None, None),
        P("latent", "dp"),
        P(),
    )

    def body(activations, owner_ids, block_mask, latent_codes, w_dec, b_dec):
        owners = mesh.shape["latent"]
        share = owner_ids.size // owners
        fits = share % 16 == 0 and owners * SPARE % 16 == 0 and w_dec.shape[1] % (128 * STACK) == 0
        pick = on_device if fits else on_device_wide
        return pick(activations, owner_ids, block_mask, latent_codes, w_dec, b_dec)

    return jax.shard_map(
        body,
        mesh=mesh,
        in_specs=placed,
        out_specs=(P(("dp", "latent"), None), P("latent", "dp")),
        check_vma=False,
    )
```

```python
import functools

import jax
import jax.numpy as jnp
from jax import lax
from jax.experimental import pallas as pl
from jax.experimental.pallas import tpu as pltpu
from jax.sharding import PartitionSpec as P

loss_scale = 1.0 / 32.0
SPARE = 2
STACK = 8
F32 = jnp.float32
BF16 = jnp.bfloat16


def mm(a, b):
    return jnp.dot(a, b, preferred_element_type=F32)


def swap_matrix(outer, inner):
    size = outer * inner * SPARE
    to = lax.broadcasted_iota(jnp.int32, (size, size), 0)
    at = lax.broadcasted_iota(jnp.int32, (size, size), 1)
    to_inner, to_outer = to // (outer * SPARE), to % (outer * SPARE) // SPARE
    at_outer, at_inner = at // (inner * SPARE), at % (inner * SPARE) // SPARE
    same = (to_inner == at_inner) & (to_outer == at_outer) & (to % SPARE == at % SPARE)
    return same.astype(F32).astype(BF16)


def pack_kernel(order, at_ref, owner_ref, mask_ref, codes_ref, *outs):
    messages, (pick_ref, pick_spare_ref, place_ref, place_spare_ref) = outs[:-4], outs[-4:]
    owners = len(messages)
    rows, visits = owner_ref.shape
    width = codes_ref.shape[1] // visits
    blocks = mask_ref.shape[1] // visits
    block = width // blocks
    main = rows * visits // owners
    slots = owners * (main + SPARE)
    apart = owner_ref[...] ^ at_ref[0]
    relative = sum(jnp.where(apart == k, p, 0) for p, k in enumerate(order))
    eye = lax.broadcasted_iota(jnp.int32, (rows, rows), 0) == lax.broadcasted_iota(jnp.int32, (rows, rows), 1)
    columns = [relative[:, g : g + 1] for g in range(visits)]
    lanes = [jnp.sum(jnp.where(eye, column, 0), axis=0, keepdims=True) for column in columns]
    column, lane = jnp.concatenate(columns, axis=0), jnp.concatenate(lanes, axis=1)
    total = rows * visits
    down = lax.broadcasted_iota(jnp.int32, (total, total), 0)
    across = lax.broadcasted_iota(jnp.int32, (total, total), 1)
    same = column == lane

    def slot_of(owner, place):
        return jnp.where(place < main, owner * main + place, owners * main + owner * SPARE + place - main)

    slot_lane = slot_of(lane, jnp.sum(jnp.where(same & (down < across), 1, 0), axis=0, keepdims=True))
    slot_column = slot_of(column, jnp.sum(jnp.where(same & (across < down), 1, 0), axis=1, keepdims=True))
    place = (lax.broadcasted_iota(jnp.int32, (slots, total), 0) == slot_lane).astype(F32)
    pick = (lax.broadcasted_iota(jnp.int32, (total, slots), 1) == slot_column).astype(F32)
    place_rows = sum(place[:, g * rows : (g + 1) * rows] for g in range(visits)).astype(BF16)
    pick_rows = sum(pick[g * rows : (g + 1) * rows, :] for g in range(visits)).astype(BF16)
    pick_ref[...] = pick_rows[:, : owners * main]
    pick_spare_ref[...] = pick_rows[:, owners * main :]
    place_ref[...] = place_rows[: owners * main, :]
    place_spare_ref[...] = place_rows[owners * main :, :]
    used = jnp.concatenate(
        [
            jnp.concatenate(
                [
                    codes_ref[:, g * width + b * block : g * width + (b + 1) * block]
                    * mask_ref[:, g * blocks + b : g * blocks + b + 1].astype(F32).astype(BF16)
                    for b in range(blocks)
                ],
                axis=1,
            )
            for g in range(visits)
        ],
        axis=0,
    )
    sorted_codes = mm(place.astype(BF16), used).astype(BF16)
    part = width // STACK
    for q in range(STACK):
        stack(messages, q, main, sorted_codes[: owners * main, q * part : (q + 1) * part])
    spare = [sorted_codes[owners * main :, q * part : (q + 1) * part] for q in range(STACK)]
    stack_spare(messages, main, jnp.concatenate(spare, axis=0))


def stack(messages, q, main, block):
    for p, message in enumerate(messages):
        message[q * main : (q + 1) * main, :] = block[p * main : (p + 1) * main, :]


def stack_spare(messages, main, spare):
    spare = mm(swap_matrix(STACK, len(messages)), spare).astype(BF16)
    for p, message in enumerate(messages):
        message[STACK * main :, :] = spare[p * STACK * SPARE : (p + 1) * STACK * SPARE, :]


def unstacked(messages, q, main):
    return jnp.concatenate([message[q * main : (q + 1) * main, :] for message in messages], axis=0)


def unstacked_spare(messages, main):
    spare = jnp.concatenate([message[STACK * main :, :] for message in messages], axis=0)
    return mm(swap_matrix(len(messages), STACK), spare).astype(BF16)


def main_of(message):
    return message.shape[0] // STACK - SPARE


def unpack_kernel(owners, *refs):
    messages, out_ref = refs[:owners], refs[owners]
    main, part = main_of(messages[0]), messages[0].shape[1]
    spares = owners * SPARE
    spare = unstacked_spare(messages, main)
    for q in range(STACK):
        out_ref[: owners * main, q * part : (q + 1) * part] = unstacked(messages, q, main)
        out_ref[owners * main :, q * part : (q + 1) * part] = spare[q * spares : (q + 1) * spares, :]


def decode_kernel(owners, codes_ref, w_ref, *rest):
    messages = rest[-owners:]
    main, part = main_of(messages[0]), messages[0].shape[1]
    spares = []
    for q in range(STACK):
        term = mm(codes_ref[...], w_ref[:, q * part : (q + 1) * part]).astype(BF16)
        stack(messages, q, main, term[: owners * main, :])
        spares.append(term[owners * main :, :])
    stack_spare(messages, main, jnp.concatenate(spares, axis=0))


def combine_kernel(owners, place_in_ref, pick_ref, pick_spare_ref, place_ref, place_spare_ref, b_ref, act_ref, *rest):
    terms, rebuilt_ref, messages = rest[:owners], rest[-owners - 1], rest[-owners:]
    main, part = main_of(messages[0]), messages[0].shape[1]
    spares = owners * SPARE
    spare_in = unstacked_spare(terms, main)
    spare_out = []
    for q in range(STACK):
        columns = slice(q * part, (q + 1) * part)
        total = mm(pick_ref[...], unstacked(terms, q, main))
        total += mm(pick_spare_ref[...], spare_in[q * spares : (q + 1) * spares, :])
        wide = b_ref[:, columns] + total
        rebuilt_ref[:, columns] = wide.astype(BF16)
        errors = (wide - act_ref[:, columns].astype(F32)).astype(BF16)
        stack(messages, q, main, mm(place_ref[...], errors).astype(BF16))
        spare_out.append(mm(place_spare_ref[...], errors).astype(BF16))
    stack_spare(messages, main, jnp.concatenate(spare_out, axis=0))


def turn_kernel(chunks, *refs):
    codes, (out_ref, spare_ref) = refs[:chunks], refs[-2:]
    main = out_ref.shape[1] // chunks
    for j in range(chunks):
        out_ref[:, j * main : (j + 1) * main] = codes[j][:main, :].astype(F32).T.astype(BF16)
    spare = jnp.concatenate([code[main:, :] for code in codes], axis=0)
    spare_ref[...] = spare.astype(F32).T.astype(BF16)


def gradient_kernel(chunks, owners, has_base, scale, codes_ref, spare_codes_ref, *refs):
    messages, base_ref, (out_ref, spare_ref) = refs[: chunks * owners], refs[chunks * owners], refs[-2:]
    main, part = main_of(messages[0]), messages[0].shape[1]
    spares = owners * SPARE
    step = pl.program_id(0)
    own = [messages[j * owners : (j + 1) * owners] for j in range(chunks)]

    @pl.when(step == 0)
    def _():
        for j in range(chunks):
            spare_ref[j] = unstacked_spare(own[j], main)

    per = out_ref.shape[1] // part
    for i in range(per):
        q = step * per + i
        at = pl.ds(pl.multiple_of(q * main, main), main)
        spare_at = pl.ds(pl.multiple_of(q * spares, spares), spares)
        columns = slice(i * part, (i + 1) * part)
        arrived = jnp.concatenate([m[at, :] for j in range(chunks) for m in own[j]], axis=0)
        spare = jnp.concatenate([spare_ref[j, spare_at, :] for j in range(chunks)], axis=0)
        total = mm(codes_ref[...], arrived) + mm(spare_codes_ref[...], spare)
        if has_base:
            total += base_ref[:, columns]
        out_ref[:, columns] = (total * scale).astype(out_ref.dtype)


ANYWHERE = pl.BlockSpec(memory_space=pl.ANY)


def whole(shape):
    return pl.BlockSpec(shape, lambda *_: (0,) * len(shape))


def params(mib):
    return pltpu.CompilerParams(vmem_limit_bytes=mib * 2**20)


def cost(flops, moved):
    return pl.CostEstimate(flops=int(flops), bytes_accessed=int(moved), transcendentals=0)


def on_device(activations, owner_ids, block_mask, latent_codes, w_dec, b_dec):
    rows, visits = owner_ids.shape
    width = latent_codes.shape[2]
    model = activations.shape[1]
    owners, groups = lax.axis_size("latent"), lax.axis_size("dp")
    main = rows * visits // owners
    slots = owners * (main + SPARE)
    depth = STACK * (main + SPARE)
    local = w_dec.shape[1]
    part = local // STACK
    place = jnp.stack([lax.axis_index("latent"), lax.axis_index("dp")])
    order = []
    for near in range(1, owners // 2 + 1):
        order += [owners - near] + ([near] if near != owners - near else [])
    order += [0]
    half = owners // 2

    def move(x, j, k):
        if j == 0 and k == 0:
            return x
        pairs = [(i, i ^ (j * owners + k)) for i in range(groups * owners)]
        return lax.ppermute(x, ("dp", "latent"), pairs)

    def move_all(messages, j):
        return [move(message, j, k) for message, k in zip(messages, order)]

    def some(shape, dtype=BF16):
        return jax.ShapeDtypeStruct(shape, dtype)

    packed = pl.pallas_call(
        functools.partial(pack_kernel, order),
        grid_spec=pltpu.PrefetchScalarGridSpec(
            num_scalar_prefetch=1,
            grid=(1,),
            in_specs=[whole((rows, visits)), whole((rows, visits * block_mask.shape[2])), whole((rows, visits * width))],
            out_specs=[whole((depth, width // STACK))] * owners
            + [whole((rows, owners * main)), whole((rows, owners * SPARE))]
            + [whole((owners * main, rows)), whole((owners * SPARE, rows))],
        ),
        out_shape=[some((depth, width // STACK))] * owners
        + [some((rows, owners * main)), some((rows, owners * SPARE))]
        + [some((owners * main, rows)), some((owners * SPARE, rows))],
        compiler_params=params(12),
        cost_estimate=cost(2 * slots * rows * visits * width, 4 * rows * visits * width),
        name="pack",
    )(place, owner_ids, block_mask.reshape(rows, -1), latent_codes.reshape(rows, -1))
    picks = packed[owners:]
    arrived = move_all(packed[:owners], 0)
    codes = [None] * groups
    codes[0] = pl.pallas_call(
        functools.partial(unpack_kernel, owners),
        out_shape=some((slots, width)),
        compiler_params=params(8),
        cost_estimate=cost(0, 4 * slots * width),
        name="unpack",
    )(*arrived)
    for j in range(1, groups):
        low = j & -j
        codes[j] = move(codes[j ^ low], low, 0)

    def decode(j, after):
        return pl.pallas_call(
            functools.partial(decode_kernel, owners),
            grid=(1,),
            in_specs=[whole((slots, width)), whole((width, local))] + [ANYWHERE] * len(after),
            out_specs=[whole((depth, part))] * owners,
            out_shape=[some((depth, part))] * owners,
            compiler_params=params(20),
            cost_estimate=cost(2 * slots * width * local, 2 * (width * local + slots * (width + local))),
            name="decode",
        )(codes[j], w_dec, *after)

    def combine(j, rebuilt, after):
        after = ([] if rebuilt is None else [rebuilt]) + after
        outs = pl.pallas_call(
            functools.partial(combine_kernel, owners),
            grid_spec=pltpu.PrefetchScalarGridSpec(
                num_scalar_prefetch=1,
                grid=(1,),
                in_specs=[whole(p.shape) for p in picks]
                + [pl.BlockSpec((1, local), lambda _, at: (0, at[1] ^ j))]
                + [pl.BlockSpec((rows, local), lambda _, at: (0, at[1] ^ j))]
                + [whole((depth, part))] * owners
                + [ANYWHERE] * len(after),
                out_specs=[pl.BlockSpec((rows, local), lambda _, at: (0, at[1] ^ j))] + [whole((depth, part))] * owners,
            ),
            out_shape=[some((rows, model))] + [some((depth, part))] * owners,
            input_output_aliases={} if rebuilt is None else {7 + owners: 0},
            compiler_params=params(16),
            cost_estimate=cost(4 * slots * rows * local, 2 * local * (2 * slots + 2 * rows)),
            name="combine",
        )(place, *picks, b_dec.reshape(1, -1), activations, *terms[j], *after)
        return outs[0], outs[1:]

    def gradient(chunks, base, scale, dtype, per, after):
        count = len(chunks)
        turned = pl.pallas_call(
            functools.partial(turn_kernel, count),
            out_shape=[some((width, count * owners * main)), some((width, count * owners * SPARE))],
            compiler_params=params(16),
            cost_estimate=cost(0, 4 * count * slots * width),
            name="turn",
        )(*[codes[j] for j in chunks])
        block = pl.BlockSpec((width, per * part), lambda q: (0, q))
        extra = ([] if base is None else [base]) + after
        return pl.pallas_call(
            functools.partial(gradient_kernel, count, owners, base is not None, scale),
            grid=(STACK // per,),
            in_specs=[whole(t.shape) for t in turned]
            + [whole((depth, part))] * (count * owners)
            + ([] if base is None else [block])
            + [ANYWHERE] * len(after),
            out_specs=block,
            out_shape=some((width, local), dtype),
            scratch_shapes=[pltpu.VMEM((count, STACK * owners * SPARE, part), BF16)],
            compiler_params=params(24),
            cost_estimate=cost(2 * count * slots * width * local, 4 * width * local),
            name="gradient",
        )(*turned, *[m for j in chunks for m in errors[j]], *extra)

    terms, errors = [None] * groups, [None] * groups
    for j in range(groups):
        terms[j] = move_all(decode(j, list(terms[j - 2][:half]) if j >= 2 else []), j)
    rebuilt = None
    for j in range(groups):
        ahead = terms[j + 1][:half] if j + 1 < groups else errors[j - 2][:half] if j >= 2 else []
        rebuilt, outgoing = combine(j, rebuilt, list(ahead))
        errors[j] = move_all(outgoing, j)
    early, last = list(range(groups - 1)), [groups - 1]
    base = gradient(early, None, 1.0, F32, 1, list(errors[groups - 1][:half]))
    return rebuilt, gradient(last, base, loss_scale, BF16, 2, [])


def on_device_wide(activations, owner_ids, block_mask, latent_codes, w_dec, b_dec):
    row_count, visit_count = owner_ids.shape
    block_count = block_mask.shape[2]
    slab_width = latent_codes.shape[2]
    block_width = slab_width // block_count
    model_width = activations.shape[1]
    owners = lax.axis_size("latent")
    groups = lax.axis_size("dp")
    capacity = row_count * visit_count // owners + SPARE
    live = block_mask.astype(latent_codes.dtype)[:, :, :, None]
    used = (latent_codes.reshape(row_count, visit_count, block_count, block_width) * live).reshape(-1, slab_width)
    onehot = (owner_ids[:, :, None] == lax.broadcasted_iota(jnp.int32, (1, 1, owners), 2)).astype(jnp.int32)
    per_row = jnp.sum(onehot, axis=1)
    before = jnp.cumsum(per_row, axis=0) - per_row
    position = jnp.sum(onehot * before[:, None, :], axis=2)
    target_slot = (owner_ids * capacity + position).reshape(-1)
    outgoing = jnp.zeros((owners * capacity, slab_width), latent_codes.dtype)
    outgoing = outgoing.at[target_slot].set(used).reshape(owners, capacity, slab_width)
    arrived = lax.all_to_all(outgoing, "latent", split_axis=0, concat_axis=0, tiled=True)
    copies = lax.all_gather(arrived, "dp", axis=0, tiled=True)
    decoded = mm(copies.reshape(-1, slab_width), w_dec).astype(BF16)
    local = w_dec.shape[1]
    returned = lax.all_to_all(
        decoded.reshape(groups * owners, capacity, local), ("dp", "latent"), split_axis=0, concat_axis=0, tiled=True
    )
    returned = returned.reshape(groups, owners * capacity, local)
    gathered = returned[:, target_slot].reshape(groups, row_count, visit_count, local)
    gathered = jnp.sum(gathered, axis=2, dtype=F32).transpose(1, 0, 2).reshape(row_count, model_width)
    rebuilt_wide = b_dec[None, :] + gathered
    errors = (rebuilt_wide - activations.astype(F32)).astype(BF16)
    parts = jnp.repeat(errors.reshape(row_count, groups, local).transpose(1, 0, 2), visit_count, axis=1)
    error_slots = jnp.zeros((groups, owners * capacity, local), BF16).at[:, target_slot].set(parts)
    error_parts = lax.all_to_all(
        error_slots.reshape(groups * owners, capacity, local), ("dp", "latent"), split_axis=0, concat_axis=0, tiled=True
    )
    gradient = jnp.einsum("nsi,nsd->id", copies, error_parts, preferred_element_type=F32) * loss_scale
    return rebuilt_wide.astype(BF16), gradient.astype(BF16)


def solution(mesh):
    placed = (
        P(("dp", "latent"), None),
        P(("dp", "latent"), None),
        P(("dp", "latent"), None, None),
        P(("dp", "latent"), None, None),
        P("latent", "dp"),
        P(),
    )

    def body(activations, owner_ids, block_mask, latent_codes, w_dec, b_dec):
        owners = mesh.shape["latent"]
        share = owner_ids.size // owners
        fits = share % 16 == 0 and owners * SPARE % 16 == 0 and w_dec.shape[1] % (128 * STACK) == 0
        fits = fits and mesh.size & (mesh.size - 1) == 0
        pick = on_device if fits else on_device_wide
        return pick(activations, owner_ids, block_mask, latent_codes, w_dec, b_dec)

    return jax.shard_map(
        body,
        mesh=mesh,
        in_specs=placed,
        out_specs=(P(("dp", "latent"), None), P("latent", "dp")),
        check_vma=False,
    )
```

```python
import functools

import jax
import jax.numpy as jnp
from jax import lax
from jax.experimental import pallas as pl
from jax.experimental.pallas import tpu as pltpu
from jax.sharding import PartitionSpec as P

loss_scale = 1.0 / 32.0
SPARE = 2
STACK = 8
SENDS = (
    ["T00", "T01", "C20", "T02", "C21", "T03", "C22", "T10", "C23", "T11", "T12", "T20"]
    + ["C30", "T13", "C31", "T21", "C32", "T22", "C33", "E00", "T23", "T30", "E01", "T31"]
    + ["T32", "E02", "T33", "E20", "E03", "E21", "E10", "E22"]
    + ["E11", "E23", "E30", "E12", "E31", "E13", "E32", "E33"]
)
WINDOW = 5
PIECES = 4
F32 = jnp.float32
BF16 = jnp.bfloat16


def mm(a, b):
    return jnp.dot(a, b, preferred_element_type=F32)


def swap_matrix(outer, inner):
    size = outer * inner * SPARE
    to = lax.broadcasted_iota(jnp.int32, (size, size), 0)
    at = lax.broadcasted_iota(jnp.int32, (size, size), 1)
    to_inner, to_outer = to // (outer * SPARE), to % (outer * SPARE) // SPARE
    at_outer, at_inner = at // (inner * SPARE), at % (inner * SPARE) // SPARE
    same = (to_inner == at_inner) & (to_outer == at_outer) & (to % SPARE == at % SPARE)
    return same.astype(F32).astype(BF16)


def pack_kernel(order, at_ref, owner_ref, mask_ref, codes_ref, *outs):
    messages, (pick_ref, pick_spare_ref, place_ref, place_spare_ref) = outs[:-4], outs[-4:]
    owners = len(messages)
    visits, rows = owner_ref.shape
    width = codes_ref.shape[1] // visits
    blocks = mask_ref.shape[0] // visits
    block = width // blocks
    main = rows * visits // owners
    slots = owners * (main + SPARE)
    apart = owner_ref[...] ^ at_ref[0]
    relative = sum(jnp.where(apart == k, p, 0) for p, k in enumerate(order))
    eye = lax.broadcasted_iota(jnp.int32, (rows, rows), 0) == lax.broadcasted_iota(jnp.int32, (rows, rows), 1)
    lanes = [relative[g : g + 1, :] for g in range(visits)]
    columns = [jnp.sum(jnp.where(eye, lane, 0), axis=1, keepdims=True) for lane in lanes]
    column, lane = jnp.concatenate(columns, axis=0), jnp.concatenate(lanes, axis=1)
    total = rows * visits
    down = lax.broadcasted_iota(jnp.int32, (total, total), 0)
    across = lax.broadcasted_iota(jnp.int32, (total, total), 1)
    same = column == lane

    def slot_of(owner, place):
        return jnp.where(place < main, owner * main + place, owners * main + owner * SPARE + place - main)

    slot_lane = slot_of(lane, jnp.sum(jnp.where(same & (down < across), 1, 0), axis=0, keepdims=True))
    slot_column = slot_of(column, jnp.sum(jnp.where(same & (across < down), 1, 0), axis=1, keepdims=True))
    place = (lax.broadcasted_iota(jnp.int32, (slots, total), 0) == slot_lane).astype(F32)
    pick = (lax.broadcasted_iota(jnp.int32, (total, slots), 1) == slot_column).astype(F32)
    place_rows = sum(place[:, g * rows : (g + 1) * rows] for g in range(visits)).astype(BF16)
    pick_rows = sum(pick[g * rows : (g + 1) * rows, :] for g in range(visits)).astype(BF16)
    pick_ref[...] = pick_rows[:, : owners * main]
    pick_spare_ref[...] = pick_rows[:, owners * main :]
    place_ref[...] = place_rows[: owners * main, :]
    place_spare_ref[...] = place_rows[owners * main :, :]
    live = mask_ref[...].astype(F32).T.astype(BF16)
    used = jnp.concatenate(
        [
            jnp.concatenate(
                [
                    codes_ref[:, g * width + b * block : g * width + (b + 1) * block] * live[:, g * blocks + b : g * blocks + b + 1]
                    for b in range(blocks)
                ],
                axis=1,
            )
            for g in range(visits)
        ],
        axis=0,
    )
    sorted_codes = mm(place.astype(BF16), used).astype(BF16)
    part = width // STACK
    for q in range(STACK):
        stack(messages, q, main, sorted_codes[: owners * main, q * part : (q + 1) * part])
    spare = [sorted_codes[owners * main :, q * part : (q + 1) * part] for q in range(STACK)]
    stack_spare(messages, main, jnp.concatenate(spare, axis=0))


def stack(messages, q, main, block):
    for p, message in enumerate(messages):
        message[q * main : (q + 1) * main, :] = block[p * main : (p + 1) * main, :]


def stack_spare(messages, main, spare):
    spare = mm(swap_matrix(STACK, len(messages)), spare).astype(BF16)
    for p, message in enumerate(messages):
        message[STACK * main :, :] = spare[p * STACK * SPARE : (p + 1) * STACK * SPARE, :]


def unstacked(messages, q, main):
    return jnp.concatenate([message[q * main : (q + 1) * main, :] for message in messages], axis=0)


def unstacked_spare(messages, main):
    spare = jnp.concatenate([message[STACK * main :, :] for message in messages], axis=0)
    return mm(swap_matrix(len(messages), STACK), spare).astype(BF16)


def main_of(message):
    return message.shape[0] // STACK - SPARE


def cut(codes, pieces):
    wide = codes.shape[1] // len(pieces)
    for i, piece in enumerate(pieces):
        piece[...] = codes[:, i * wide : (i + 1) * wide]


def joined(pieces):
    return jnp.concatenate([piece[...] for piece in pieces], axis=1)


def unpack_kernel(owners, *refs):
    messages, out_ref, pieces = refs[:owners], refs[-1 - PIECES], refs[-PIECES:]
    main, part = main_of(messages[0]), messages[0].shape[1]
    spares = owners * SPARE
    spare = unstacked_spare(messages, main)
    for q in range(STACK):
        out_ref[: owners * main, q * part : (q + 1) * part] = unstacked(messages, q, main)
        out_ref[owners * main :, q * part : (q + 1) * part] = spare[q * spares : (q + 1) * spares, :]
    cut(out_ref[...], pieces)


def decode_kernel(owners, given, w_ref, *refs):
    codes = joined(refs[:given])
    messages, copies = refs[given : given + owners], refs[given + owners :]
    if copies:
        cut(codes, copies)
    main, part = main_of(messages[0]), messages[0].shape[1]
    spares = []
    for q in range(STACK):
        term = mm(codes, w_ref[:, q * part : (q + 1) * part]).astype(BF16)
        stack(messages, q, main, term[: owners * main, :])
        spares.append(term[owners * main :, :])
    stack_spare(messages, main, jnp.concatenate(spares, axis=0))


def touch_kernel(*refs):
    refs[-1][...] = jnp.zeros_like(refs[-1])


def combine_kernel(owners, place_in_ref, pick_ref, pick_spare_ref, place_ref, place_spare_ref, b_ref, act_ref, *rest):
    terms, rebuilt_ref, messages = rest[:owners], rest[-owners - 1], rest[-owners:]
    main, part = main_of(messages[0]), messages[0].shape[1]
    spares = owners * SPARE
    spare_in = unstacked_spare(terms, main)
    spare_out = []
    for q in range(STACK):
        columns = slice(q * part, (q + 1) * part)
        total = mm(pick_ref[...], unstacked(terms, q, main))
        total += mm(pick_spare_ref[...], spare_in[q * spares : (q + 1) * spares, :])
        wide = b_ref[:, columns] + total
        rebuilt_ref[:, columns] = wide.astype(BF16)
        errors = (wide - act_ref[:, columns].astype(F32)).astype(BF16)
        stack(messages, q, main, mm(place_ref[...], errors).astype(BF16))
        spare_out.append(mm(place_spare_ref[...], errors).astype(BF16))
    stack_spare(messages, main, jnp.concatenate(spare_out, axis=0))


def turn_kernel(counts, scale, *refs):
    chunks, (out_ref, spare_ref) = len(counts), refs[-2:]
    codes = [joined(refs[sum(counts[:j]) : sum(counts[: j + 1])]) for j in range(chunks)]
    main = out_ref.shape[1] // chunks
    for j in range(chunks):
        out_ref[:, j * main : (j + 1) * main] = (codes[j][:main, :].astype(F32) * scale).T.astype(BF16)
    spare = jnp.concatenate([code[main:, :] for code in codes], axis=0)
    spare_ref[...] = (spare.astype(F32) * scale).T.astype(BF16)


def gradient_kernel(chunks, owners, has_base, codes_ref, spare_codes_ref, *refs):
    messages, base_ref, (out_ref, spare_ref) = refs[: chunks * owners], refs[chunks * owners], refs[-2:]
    main, part = main_of(messages[0]), messages[0].shape[1]
    spares = owners * SPARE
    step = pl.program_id(0)
    own = [messages[j * owners : (j + 1) * owners] for j in range(chunks)]

    @pl.when(step == 0)
    def _():
        for j in range(chunks):
            spare_ref[j] = unstacked_spare(own[j], main)

    per = out_ref.shape[1] // part
    for i in range(per):
        q = step * per + i
        at = pl.ds(pl.multiple_of(q * main, main), main)
        spare_at = pl.ds(pl.multiple_of(q * spares, spares), spares)
        columns = slice(i * part, (i + 1) * part)
        arrived = jnp.concatenate([m[at, :] for j in range(chunks) for m in own[j]], axis=0)
        spare = jnp.concatenate([spare_ref[j, spare_at, :] for j in range(chunks)], axis=0)
        total = mm(codes_ref[...], arrived) + mm(spare_codes_ref[...], spare)
        if has_base:
            total += base_ref[:, columns]
        out_ref[:, columns] = total.astype(out_ref.dtype)


def gate_kernel(*_):
    pass


ANYWHERE = pl.BlockSpec(memory_space=pl.ANY)


def whole(shape):
    return pl.BlockSpec(shape, lambda *_: (0,) * len(shape))


def params(mib):
    return pltpu.CompilerParams(vmem_limit_bytes=mib * 2**20)


def cost(flops, moved):
    return pl.CostEstimate(flops=int(flops), bytes_accessed=int(moved), transcendentals=0)


def on_device(activations, owner_ids, block_mask, latent_codes, w_dec, b_dec):
    rows, visits = owner_ids.shape
    width = latent_codes.shape[2]
    model = activations.shape[1]
    owners, groups = lax.axis_size("latent"), lax.axis_size("dp")
    main = rows * visits // owners
    slots = owners * (main + SPARE)
    depth = STACK * (main + SPARE)
    local = w_dec.shape[1]
    part = local // STACK
    position = jnp.stack([lax.axis_index("latent"), lax.axis_index("dp")])
    order = [7, 1, 6, 2, 5, 3, 4, 0]

    def move(x, j, k):
        if j == 0 and k == 0:
            return x
        pairs = [(i, i ^ (j * owners + k)) for i in range(groups * owners)]
        return lax.ppermute(x, ("dp", "latent"), pairs)

    def move_all(messages, j):
        return [move(message, j, k) for message, k in zip(messages, order)]

    def some(shape, dtype=BF16):
        return jax.ShapeDtypeStruct(shape, dtype)

    packed = pl.pallas_call(
        functools.partial(pack_kernel, order),
        grid_spec=pltpu.PrefetchScalarGridSpec(
            num_scalar_prefetch=1,
            grid=(1,),
            in_specs=[whole((visits, rows)), whole((visits * block_mask.shape[2], rows)), whole((rows, visits * width))],
            out_specs=[whole((depth, width // STACK))] * owners
            + [whole((rows, owners * main)), whole((rows, owners * SPARE))]
            + [whole((owners * main, rows)), whole((owners * SPARE, rows))],
        ),
        out_shape=[some((depth, width // STACK))] * owners
        + [some((rows, owners * main)), some((rows, owners * SPARE))]
        + [some((owners * main, rows)), some((owners * SPARE, rows))],
        compiler_params=params(12),
        cost_estimate=cost(2 * slots * rows * visits * width, 0),
        name="pack",
    )(position, owner_ids.T, block_mask.transpose(1, 2, 0).reshape(-1, rows), latent_codes.reshape(rows, -1))
    picks = packed[owners:]
    arrived = move_all(packed[:owners], 0)
    touched = pl.pallas_call(
        touch_kernel,
        in_specs=[whole(w_dec.shape), ANYWHERE],
        out_shape=some((8, 128), F32),
        compiler_params=params(12),
        cost_estimate=cost(0, 2 * width * local),
        name="touch",
    )(w_dec, arrived[0])
    piece = (slots, width // PIECES)
    own_codes, *sent_codes = pl.pallas_call(
        functools.partial(unpack_kernel, owners),
        in_specs=[whole((depth, width // STACK))] * owners + [ANYWHERE],
        out_shape=[some((slots, width))] + [some(piece)] * PIECES,
        compiler_params=params(8),
        cost_estimate=cost(0, 4 * slots * width),
        name="unpack",
    )(*arrived, touched)
    codes = [[own_codes], [move(own_codes, 1, 0)], [None] * PIECES, [None] * PIECES]

    def decode(j):
        copied = [piece] * PIECES if j == 2 else []
        return pl.pallas_call(
            functools.partial(decode_kernel, owners, len(codes[j])),
            in_specs=[whole((width, local))] + [whole(c.shape) for c in codes[j]],
            out_specs=[whole((depth, part))] * owners + [whole(c) for c in copied],
            out_shape=[some((depth, part))] * owners + [some(c) for c in copied],
            compiler_params=params(16),
            cost_estimate=cost(2 * slots * width * local, 2 * (width * local + slots * (width + local))),
            name="decode",
        )(w_dec, *codes[j])

    def combine(j, rebuilt):
        after = [] if rebuilt is None else [rebuilt]
        outs = pl.pallas_call(
            functools.partial(combine_kernel, owners),
            grid_spec=pltpu.PrefetchScalarGridSpec(
                num_scalar_prefetch=1,
                grid=(1,),
                in_specs=[whole(p.shape) for p in picks]
                + [pl.BlockSpec((1, local), lambda _, at: (0, at[1] ^ j))]
                + [pl.BlockSpec((rows, local), lambda _, at: (0, at[1] ^ j))]
                + [whole((depth, part))] * owners
                + [ANYWHERE] * len(after),
                out_specs=[pl.BlockSpec((rows, local), lambda _, at: (0, at[1] ^ j))] + [whole((depth, part))] * owners,
            ),
            out_shape=[some((rows, model))] + [some((depth, part))] * owners,
            input_output_aliases={7 + owners: 0} if after else {},
            compiler_params=params(16),
            cost_estimate=cost(4 * slots * rows * local, 2 * local * (2 * slots + 2 * rows)),
            name="combine",
        )(position, *picks, b_dec.reshape(1, -1), activations, *terms[j], *after)
        return outs[0], outs[1:]

    def gradient(chunks, base, dtype, per, after):
        count = len(chunks)
        pieces = [c for j in chunks for c in codes[j]]
        turned = pl.pallas_call(
            functools.partial(turn_kernel, [len(codes[j]) for j in chunks], loss_scale),
            in_specs=[whole(c.shape) for c in pieces],
            out_shape=[some((width, count * owners * main)), some((width, count * owners * SPARE))],
            compiler_params=params(16),
            cost_estimate=cost(0, 4 * count * slots * width),
            name="turn",
        )(*pieces)
        block = pl.BlockSpec((width, per * part), lambda q: (0, q))
        extra = ([] if base is None else [base]) + after
        return pl.pallas_call(
            functools.partial(gradient_kernel, count, owners, base is not None),
            grid=(STACK // per,),
            in_specs=[whole(t.shape) for t in turned]
            + [whole((depth, part))] * (count * owners)
            + ([] if base is None else [block])
            + [ANYWHERE] * len(after),
            out_specs=block,
            out_shape=some((width, local), dtype),
            scratch_shapes=[pltpu.VMEM((count, STACK * owners * SPARE, part), BF16)],
            compiler_params=params(24),
            cost_estimate=cost(2 * count * slots * width * local, 4 * width * local),
            name="gradient",
        )(*turned, *[m for j in chunks for m in errors[j]], *extra)

    def gate(messages, after):
        held = pl.pallas_call(
            gate_kernel,
            in_specs=[ANYWHERE] * (len(messages) + len(after)),
            out_specs=[ANYWHERE] * len(messages),
            out_shape=[some(m.shape) for m in messages],
            input_output_aliases={i: i for i in range(len(messages))},
            compiler_params=params(1),
            cost_estimate=cost(0, 0),
            name="gate",
        )(*messages, *after)
        return list(held)

    terms, errors, leaving = [[None] * owners for _ in range(groups)], [[None] * owners for _ in range(groups)], {}
    rebuilt, arrivals, held = None, list(codes[1]), []
    for kind, j, at in SENDS:
        j, at = int(j), int(at)
        if kind == "C":
            chunk, messages = codes[j], [(sent_codes[at], 2, 0, at) if j == 2 else (leaving["T", 2][owners + at], 1, 0, at)]
        else:
            chunk = (terms if kind == "T" else errors)[j]
            if (kind, j) not in leaving:
                if kind == "T":
                    leaving[kind, j] = decode(j)
                else:
                    rebuilt, leaving[kind, j] = combine(j, rebuilt)
            messages = [(leaving[kind, j][p], j, order[p], p) for p in (2 * at, 2 * at + 1)]
        for message, across, along, place in messages:
            if across or along:
                (message,) = held = gate([message], arrivals[-WINDOW:][:1] * (len(arrivals) >= WINDOW) + held)
                message = move(message, across, along)
                arrivals.append(message)
            chunk[place] = message
    base = gradient([0, 2, 1], None, F32, 1, held[:1])
    return rebuilt, gradient([3], base, BF16, 2, [])


def on_device_wide(activations, owner_ids, block_mask, latent_codes, w_dec, b_dec):
    row_count, visit_count = owner_ids.shape
    block_count = block_mask.shape[2]
    slab_width = latent_codes.shape[2]
    block_width = slab_width // block_count
    model_width = activations.shape[1]
    owners = lax.axis_size("latent")
    groups = lax.axis_size("dp")
    capacity = row_count * visit_count // owners + SPARE
    live = block_mask.astype(latent_codes.dtype)[:, :, :, None]
    used = (latent_codes.reshape(row_count, visit_count, block_count, block_width) * live).reshape(-1, slab_width)
    onehot = (owner_ids[:, :, None] == lax.broadcasted_iota(jnp.int32, (1, 1, owners), 2)).astype(jnp.int32)
    per_row = jnp.sum(onehot, axis=1)
    before = jnp.cumsum(per_row, axis=0) - per_row
    position = jnp.sum(onehot * before[:, None, :], axis=2)
    target_slot = (owner_ids * capacity + position).reshape(-1)
    outgoing = jnp.zeros((owners * capacity, slab_width), latent_codes.dtype)
    outgoing = outgoing.at[target_slot].set(used).reshape(owners, capacity, slab_width)
    arrived = lax.all_to_all(outgoing, "latent", split_axis=0, concat_axis=0, tiled=True)
    copies = lax.all_gather(arrived, "dp", axis=0, tiled=True)
    decoded = mm(copies.reshape(-1, slab_width), w_dec).astype(BF16)
    local = w_dec.shape[1]
    returned = lax.all_to_all(
        decoded.reshape(groups * owners, capacity, local), ("dp", "latent"), split_axis=0, concat_axis=0, tiled=True
    )
    returned = returned.reshape(groups, owners * capacity, local)
    gathered = returned[:, target_slot].reshape(groups, row_count, visit_count, local)
    gathered = jnp.sum(gathered, axis=2, dtype=F32).transpose(1, 0, 2).reshape(row_count, model_width)
    rebuilt_wide = b_dec[None, :] + gathered
    errors = (rebuilt_wide - activations.astype(F32)).astype(BF16)
    parts = jnp.repeat(errors.reshape(row_count, groups, local).transpose(1, 0, 2), visit_count, axis=1)
    error_slots = jnp.zeros((groups, owners * capacity, local), BF16).at[:, target_slot].set(parts)
    error_parts = lax.all_to_all(
        error_slots.reshape(groups * owners, capacity, local), ("dp", "latent"), split_axis=0, concat_axis=0, tiled=True
    )
    gradient = jnp.einsum("nsi,nsd->id", copies, error_parts, preferred_element_type=F32) * loss_scale
    return rebuilt_wide.astype(BF16), gradient.astype(BF16)


def solution(mesh):
    placed = (
        P(("dp", "latent"), None),
        P(("dp", "latent"), None),
        P(("dp", "latent"), None, None),
        P(("dp", "latent"), None, None),
        P("latent", "dp"),
        P(),
    )

    def body(activations, owner_ids, block_mask, latent_codes, w_dec, b_dec):
        owners = mesh.shape["latent"]
        share = owner_ids.size // owners
        fits = share % 16 == 0 and owners * SPARE % 16 == 0 and w_dec.shape[1] % (128 * STACK) == 0
        fits = fits and owners == 8 and mesh.shape["dp"] == 4
        pick = on_device if fits else on_device_wide
        return pick(activations, owner_ids, block_mask, latent_codes, w_dec, b_dec)

    return jax.shard_map(
        body,
        mesh=mesh,
        in_specs=placed,
        out_specs=(P(("dp", "latent"), None), P("latent", "dp")),
        check_vma=False,
    )
```

```python
import functools

import jax
import jax.numpy as jnp
from jax import lax
from jax.experimental import pallas as pl
from jax.experimental.pallas import tpu as pltpu
from jax.sharding import PartitionSpec as P

loss_scale = 1.0 / 32.0
SPARE = 2
STACK = 8
SENDS = (
    ["T00", "T01", "C20", "T02", "C21", "T03", "C22", "T10", "C23", "T11", "T12", "T20", "T13", "C30", "T21", "C31"]
    + ["T22", "C32", "E00", "C33", "T23", "E01", "T30", "T31", "E02", "T32", "E03", "T33", "E20", "E10", "E21", "E22"]
    + ["E11", "E23", "E12", "E30", "E31", "E13", "E32", "E33"]
)
WINDOW = 5
PIECES = 4
F32 = jnp.float32
BF16 = jnp.bfloat16


def mm(a, b):
    return jnp.dot(a, b, preferred_element_type=F32)


def swap_matrix(outer, inner):
    size = outer * inner * SPARE
    to = lax.broadcasted_iota(jnp.int32, (size, size), 0)
    at = lax.broadcasted_iota(jnp.int32, (size, size), 1)
    to_inner, to_outer = to // (outer * SPARE), to % (outer * SPARE) // SPARE
    at_outer, at_inner = at // (inner * SPARE), at % (inner * SPARE) // SPARE
    same = (to_inner == at_inner) & (to_outer == at_outer) & (to % SPARE == at % SPARE)
    return same.astype(F32).astype(BF16)


def pack_kernel(order, at_ref, owner_ref, mask_ref, codes_ref, *outs):
    messages, (pick_ref, pick_spare_ref, place_ref, place_spare_ref) = outs[:-4], outs[-4:]
    owners = len(messages)
    visits, rows = owner_ref.shape
    width = codes_ref.shape[1] // visits
    blocks = mask_ref.shape[0] // visits
    block = width // blocks
    main = rows * visits // owners
    slots = owners * (main + SPARE)
    apart = owner_ref[...] ^ at_ref[0]
    relative = sum(jnp.where(apart == k, p, 0) for p, k in enumerate(order))
    eye = lax.broadcasted_iota(jnp.int32, (rows, rows), 0) == lax.broadcasted_iota(jnp.int32, (rows, rows), 1)
    lanes = [relative[g : g + 1, :] for g in range(visits)]
    columns = [jnp.sum(jnp.where(eye, lane, 0), axis=1, keepdims=True) for lane in lanes]
    column, lane = jnp.concatenate(columns, axis=0), jnp.concatenate(lanes, axis=1)
    total = rows * visits
    down = lax.broadcasted_iota(jnp.int32, (total, total), 0)
    across = lax.broadcasted_iota(jnp.int32, (total, total), 1)
    same = column == lane

    def slot_of(owner, place):
        return jnp.where(place < main, owner * main + place, owners * main + owner * SPARE + place - main)

    slot_lane = slot_of(lane, jnp.sum(jnp.where(same & (down < across), 1, 0), axis=0, keepdims=True))
    slot_column = slot_of(column, jnp.sum(jnp.where(same & (across < down), 1, 0), axis=1, keepdims=True))
    place = (lax.broadcasted_iota(jnp.int32, (slots, total), 0) == slot_lane).astype(F32)
    pick = (lax.broadcasted_iota(jnp.int32, (total, slots), 1) == slot_column).astype(F32)
    place_rows = sum(place[:, g * rows : (g + 1) * rows] for g in range(visits)).astype(BF16)
    pick_rows = sum(pick[g * rows : (g + 1) * rows, :] for g in range(visits)).astype(BF16)
    pick_ref[...] = pick_rows[:, : owners * main]
    pick_spare_ref[...] = pick_rows[:, owners * main :]
    place_ref[...] = place_rows[: owners * main, :]
    place_spare_ref[...] = place_rows[owners * main :, :]
    live = mask_ref[...].astype(F32).T.astype(BF16)
    used = jnp.concatenate(
        [
            jnp.concatenate(
                [
                    codes_ref[:, g * width + b * block : g * width + (b + 1) * block] * live[:, g * blocks + b : g * blocks + b + 1]
                    for b in range(blocks)
                ],
                axis=1,
            )
            for g in range(visits)
        ],
        axis=0,
    )
    sorted_codes = mm(place.astype(BF16), used).astype(BF16)
    part = width // STACK
    for q in range(STACK):
        stack(messages, q, main, sorted_codes[: owners * main, q * part : (q + 1) * part])
    spare = [sorted_codes[owners * main :, q * part : (q + 1) * part] for q in range(STACK)]
    stack_spare(messages, main, jnp.concatenate(spare, axis=0))


def stack(messages, q, main, block):
    for p, message in enumerate(messages):
        message[q * main : (q + 1) * main, :] = block[p * main : (p + 1) * main, :]


def stack_spare(messages, main, spare):
    spare = mm(swap_matrix(STACK, len(messages)), spare).astype(BF16)
    for p, message in enumerate(messages):
        message[STACK * main :, :] = spare[p * STACK * SPARE : (p + 1) * STACK * SPARE, :]


def unstacked(messages, q, main):
    return jnp.concatenate([message[q * main : (q + 1) * main, :] for message in messages], axis=0)


def unstacked_spare(messages, main):
    spare = jnp.concatenate([message[STACK * main :, :] for message in messages], axis=0)
    return mm(swap_matrix(len(messages), STACK), spare).astype(BF16)


def main_of(message):
    return message.shape[0] // STACK - SPARE


def cut(codes, pieces):
    wide = codes.shape[1] // len(pieces)
    for i, piece in enumerate(pieces):
        piece[...] = codes[:, i * wide : (i + 1) * wide]


def joined(pieces):
    return jnp.concatenate([piece[...] for piece in pieces], axis=1)


def unpack_kernel(owners, *refs):
    messages, out_ref, pieces = refs[:owners], refs[-1 - PIECES], refs[-PIECES:]
    main, part = main_of(messages[0]), messages[0].shape[1]
    spares = owners * SPARE
    spare = unstacked_spare(messages, main)
    for q in range(STACK):
        out_ref[: owners * main, q * part : (q + 1) * part] = unstacked(messages, q, main)
        out_ref[owners * main :, q * part : (q + 1) * part] = spare[q * spares : (q + 1) * spares, :]
    cut(out_ref[...], pieces)


def decode_kernel(owners, given, w_ref, *refs):
    codes = joined(refs[:given])
    messages, copies = refs[given : given + owners], refs[given + owners :]
    if copies:
        cut(codes, copies)
    main, part = main_of(messages[0]), messages[0].shape[1]
    spares = []
    for q in range(STACK):
        term = mm(codes, w_ref[:, q * part : (q + 1) * part]).astype(BF16)
        stack(messages, q, main, term[: owners * main, :])
        spares.append(term[owners * main :, :])
    stack_spare(messages, main, jnp.concatenate(spares, axis=0))


def touch_kernel(*refs):
    refs[-1][...] = jnp.zeros_like(refs[-1])


def combine_kernel(owners, place_in_ref, pick_ref, pick_spare_ref, place_ref, place_spare_ref, b_ref, act_ref, *rest):
    terms, rebuilt_ref, messages = rest[:owners], rest[-owners - 1], rest[-owners:]
    main, part = main_of(messages[0]), messages[0].shape[1]
    spares = owners * SPARE
    spare_in = unstacked_spare(terms, main)
    spare_out = []
    for q in range(STACK):
        columns = slice(q * part, (q + 1) * part)
        total = mm(pick_ref[...], unstacked(terms, q, main))
        total += mm(pick_spare_ref[...], spare_in[q * spares : (q + 1) * spares, :])
        wide = b_ref[:, columns] + total
        rebuilt_ref[:, columns] = wide.astype(BF16)
        errors = (wide - act_ref[:, columns].astype(F32)).astype(BF16)
        stack(messages, q, main, mm(place_ref[...], errors).astype(BF16))
        spare_out.append(mm(place_spare_ref[...], errors).astype(BF16))
    stack_spare(messages, main, jnp.concatenate(spare_out, axis=0))


def turn_kernel(counts, owners, main, scale, picked, *refs):
    codes, out_ref = [], refs[-1]
    for j in range(len(counts)):
        codes.append(joined(refs[sum(counts[:j]) : sum(counts[: j + 1])]).astype(F32) * scale)
    at = 0
    for code, (_, first, count) in zip(codes, picked):
        out_ref[:, at : at + count * main] = code[first * main : (first + count) * main, :].T.astype(BF16)
        at += count * main
    base = owners * main
    spare = [code[base + f * SPARE : base + (f + n) * SPARE, :] for code, (_, f, n) in zip(codes, picked)]
    out_ref[:, at:] = jnp.concatenate(spare, axis=0).T.astype(BF16)


def gradient_kernel(counts, last, codes_ref, *refs):
    own = [refs[sum(counts[:i]) : sum(counts[: i + 1])] for i in range(len(counts))]
    refs = refs[sum(counts) :]
    main, part = main_of(own[0][0]), own[0][0].shape[1]
    if last:
        base_ref, out_ref, *spare_refs, block_ref, sems = refs
    else:
        out_ref, *spare_refs = refs[-1 - len(counts) :]
    for messages, spare_ref in zip(own, spare_refs):
        spare_ref[...] = unstacked_spare(messages, main).astype(F32)

    def columns_of(q):
        return pl.ds(pl.multiple_of(q * part, part), part)

    def copy_of(q):
        return pltpu.make_async_copy(block_ref.at[:, columns_of(q)], out_ref.at[:, columns_of(q)], sems.at[q])

    def block(q, _):
        at = pl.ds(pl.multiple_of(q * main, main), main)
        arrived = [m[at, :] for messages in own for m in messages]
        spare = [
            ref[pl.ds(pl.multiple_of(q * n * SPARE, n * SPARE), n * SPARE), :] for n, ref in zip(counts, spare_refs)
        ]
        total = mm(codes_ref[...], jnp.concatenate(arrived + [jnp.concatenate(spare, axis=0).astype(BF16)], axis=0))
        if last:
            block_ref[:, columns_of(q)] = (total + base_ref[:, columns_of(q)]).astype(BF16)
            copy_of(q).start()
        else:
            out_ref[:, columns_of(q)] = total
        return _

    lax.fori_loop(0, STACK, block, 0)
    if last:
        for q in range(STACK):
            copy_of(q).wait()


def gate_kernel(*_):
    pass


ANYWHERE = pl.BlockSpec(memory_space=pl.ANY)


def whole(shape):
    return pl.BlockSpec(shape, lambda *_: (0,) * len(shape))


def params(mib):
    return pltpu.CompilerParams(vmem_limit_bytes=mib * 2**20)


def cost(flops, moved):
    return pl.CostEstimate(flops=int(flops), bytes_accessed=int(moved), transcendentals=0)


def on_device(activations, owner_ids, block_mask, latent_codes, w_dec, b_dec):
    rows, visits = owner_ids.shape
    width = latent_codes.shape[2]
    model = activations.shape[1]
    owners, groups = lax.axis_size("latent"), lax.axis_size("dp")
    main = rows * visits // owners
    slots = owners * (main + SPARE)
    depth = STACK * (main + SPARE)
    local = w_dec.shape[1]
    part = local // STACK
    position = jnp.stack([lax.axis_index("latent"), lax.axis_index("dp")])
    order = [4, 3, 5, 2, 6, 1, 7, 0]

    def move(x, j, k):
        if j == 0 and k == 0:
            return x
        pairs = [(i, i ^ (j * owners + k)) for i in range(groups * owners)]
        return lax.ppermute(x, ("dp", "latent"), pairs)

    def move_all(messages, j):
        return [move(message, j, k) for message, k in zip(messages, order)]

    def some(shape, dtype=BF16):
        return jax.ShapeDtypeStruct(shape, dtype)

    packed = pl.pallas_call(
        functools.partial(pack_kernel, order),
        grid_spec=pltpu.PrefetchScalarGridSpec(
            num_scalar_prefetch=1,
            grid=(1,),
            in_specs=[whole((visits, rows)), whole((visits * block_mask.shape[2], rows)), whole((rows, visits * width))],
            out_specs=[whole((depth, width // STACK))] * owners
            + [whole((rows, owners * main)), whole((rows, owners * SPARE))]
            + [whole((owners * main, rows)), whole((owners * SPARE, rows))],
        ),
        out_shape=[some((depth, width // STACK))] * owners
        + [some((rows, owners * main)), some((rows, owners * SPARE))]
        + [some((owners * main, rows)), some((owners * SPARE, rows))],
        compiler_params=params(12),
        cost_estimate=cost(2 * slots * rows * visits * width, 0),
        name="pack",
    )(position, owner_ids.T, block_mask.transpose(1, 2, 0).reshape(-1, rows), latent_codes.reshape(rows, -1))
    picks = packed[owners:]
    arrived = move_all(packed[:owners], 0)
    touched = pl.pallas_call(
        touch_kernel,
        in_specs=[whole(w_dec.shape), ANYWHERE],
        out_shape=some((8, 128), F32),
        compiler_params=params(12),
        cost_estimate=cost(0, 2 * width * local),
        name="touch",
    )(w_dec, arrived[0])
    piece = (slots, width // PIECES)
    own_codes, *sent_codes = pl.pallas_call(
        functools.partial(unpack_kernel, owners),
        in_specs=[whole((depth, width // STACK))] * owners + [ANYWHERE],
        out_shape=[some((slots, width))] + [some(piece)] * PIECES,
        compiler_params=params(8),
        cost_estimate=cost(0, 4 * slots * width),
        name="unpack",
    )(*arrived, touched)
    codes = [[own_codes], [move(own_codes, 1, 0)], [None] * PIECES, [None] * PIECES]

    def decode(j):
        copied = [piece] * PIECES if j == 2 else []
        return pl.pallas_call(
            functools.partial(decode_kernel, owners, len(codes[j])),
            in_specs=[whole((width, local))] + [whole(c.shape) for c in codes[j]],
            out_specs=[whole((depth, part))] * owners + [whole(c) for c in copied],
            out_shape=[some((depth, part))] * owners + [some(c) for c in copied],
            compiler_params=params(16),
            cost_estimate=cost(2 * slots * width * local, 2 * (width * local + slots * (width + local))),
            name="decode",
        )(w_dec, *codes[j])

    def combine(j, rebuilt):
        after = [] if rebuilt is None else [rebuilt]
        outs = pl.pallas_call(
            functools.partial(combine_kernel, owners),
            grid_spec=pltpu.PrefetchScalarGridSpec(
                num_scalar_prefetch=1,
                grid=(1,),
                in_specs=[whole(p.shape) for p in picks]
                + [pl.BlockSpec((1, local), lambda _, at: (0, at[1] ^ j))]
                + [pl.BlockSpec((rows, local), lambda _, at: (0, at[1] ^ j))]
                + [whole((depth, part))] * owners
                + [ANYWHERE] * len(after),
                out_specs=[pl.BlockSpec((rows, local), lambda _, at: (0, at[1] ^ j))] + [whole((depth, part))] * owners,
            ),
            out_shape=[some((rows, model))] + [some((depth, part))] * owners,
            input_output_aliases={7 + owners: 0} if after else {},
            compiler_params=params(16),
            cost_estimate=cost(4 * slots * rows * local, 2 * local * (2 * slots + 2 * rows)),
            name="combine",
        )(position, *picks, b_dec.reshape(1, -1), activations, *terms[j], *after)
        return outs[0], outs[1:]

    def gradient(picked, base, after):
        counts = [n for _, _, n in picked]
        depths = sum(counts) * (main + SPARE)
        pieces = [c for j, _, _ in picked for c in codes[j]]
        turned = pl.pallas_call(
            functools.partial(turn_kernel, [len(codes[j]) for j, _, _ in picked], owners, main, loss_scale, picked),
            in_specs=[whole(c.shape) for c in pieces],
            out_shape=some((width, depths)),
            compiler_params=params(16),
            cost_estimate=cost(0, 4 * width * depths),
            name="turn",
        )(*pieces)
        last = base is not None
        spare = [pltpu.VMEM((STACK * n * SPARE, part), F32) for n in counts]
        buffers = [pltpu.VMEM((width, local), BF16), pltpu.SemaphoreType.DMA((STACK,))] if last else []
        return pl.pallas_call(
            functools.partial(gradient_kernel, counts, last),
            in_specs=[whole(turned.shape)]
            + [whole((depth, part))] * sum(counts)
            + [whole((width, local))] * last
            + [ANYWHERE] * len(after),
            out_specs=ANYWHERE if last else whole((width, local)),
            out_shape=some((width, local), BF16 if last else F32),
            scratch_shapes=spare + buffers,
            compiler_params=params(24),
            cost_estimate=cost(2 * depths * width * local, 4 * width * local),
            name="gradient",
        )(turned, *[m for j, f, n in picked for m in errors[j][f : f + n]], *([base] if last else []), *after)

    def gate(messages, after):
        held = pl.pallas_call(
            gate_kernel,
            in_specs=[ANYWHERE] * (len(messages) + len(after)),
            out_specs=[ANYWHERE] * len(messages),
            out_shape=[some(m.shape) for m in messages],
            input_output_aliases={i: i for i in range(len(messages))},
            compiler_params=params(1),
            cost_estimate=cost(0, 0),
            name="gate",
        )(*messages, *after)
        return list(held)

    terms, errors, leaving = [[None] * owners for _ in range(groups)], [[None] * owners for _ in range(groups)], {}
    rebuilt, arrivals, held = None, list(codes[1]), []
    for kind, j, at in SENDS:
        j, at = int(j), int(at)
        if kind == "C":
            chunk, messages = codes[j], [(sent_codes[at], 2, 0, at) if j == 2 else (leaving["T", 2][owners + at], 1, 0, at)]
        else:
            chunk = (terms if kind == "T" else errors)[j]
            if (kind, j) not in leaving:
                if kind == "T":
                    leaving[kind, j] = decode(j)
                else:
                    rebuilt, leaving[kind, j] = combine(j, rebuilt)
            messages = [(leaving[kind, j][p], j, order[p], p) for p in (2 * at, 2 * at + 1)]
        for message, across, along, place in messages:
            if across or along:
                (message,) = held = gate([message], arrivals[-WINDOW:][:1] * (len(arrivals) >= WINDOW) + held)
                message = move(message, across, along)
                arrivals.append(message)
            chunk[place] = message
    half = owners // 2
    base = gradient([(0, 0, owners), (2, 0, owners), (1, 0, owners), (3, 0, half)], None, held)
    return rebuilt, gradient([(3, half, owners - half)], base, [])


def on_device_wide(activations, owner_ids, block_mask, latent_codes, w_dec, b_dec):
    row_count, visit_count = owner_ids.shape
    block_count = block_mask.shape[2]
    slab_width = latent_codes.shape[2]
    block_width = slab_width // block_count
    model_width = activations.shape[1]
    owners = lax.axis_size("latent")
    groups = lax.axis_size("dp")
    capacity = row_count * visit_count // owners + SPARE
    live = block_mask.astype(latent_codes.dtype)[:, :, :, None]
    used = (latent_codes.reshape(row_count, visit_count, block_count, block_width) * live).reshape(-1, slab_width)
    onehot = (owner_ids[:, :, None] == lax.broadcasted_iota(jnp.int32, (1, 1, owners), 2)).astype(jnp.int32)
    per_row = jnp.sum(onehot, axis=1)
    before = jnp.cumsum(per_row, axis=0) - per_row
    position = jnp.sum(onehot * before[:, None, :], axis=2)
    target_slot = (owner_ids * capacity + position).reshape(-1)
    outgoing = jnp.zeros((owners * capacity, slab_width), latent_codes.dtype)
    outgoing = outgoing.at[target_slot].set(used).reshape(owners, capacity, slab_width)
    arrived = lax.all_to_all(outgoing, "latent", split_axis=0, concat_axis=0, tiled=True)
    copies = lax.all_gather(arrived, "dp", axis=0, tiled=True)
    decoded = mm(copies.reshape(-1, slab_width), w_dec).astype(BF16)
    local = w_dec.shape[1]
    returned = lax.all_to_all(
        decoded.reshape(groups * owners, capacity, local), ("dp", "latent"), split_axis=0, concat_axis=0, tiled=True
    )
    returned = returned.reshape(groups, owners * capacity, local)
    gathered = returned[:, target_slot].reshape(groups, row_count, visit_count, local)
    gathered = jnp.sum(gathered, axis=2, dtype=F32).transpose(1, 0, 2).reshape(row_count, model_width)
    rebuilt_wide = b_dec[None, :] + gathered
    errors = (rebuilt_wide - activations.astype(F32)).astype(BF16)
    parts = jnp.repeat(errors.reshape(row_count, groups, local).transpose(1, 0, 2), visit_count, axis=1)
    error_slots = jnp.zeros((groups, owners * capacity, local), BF16).at[:, target_slot].set(parts)
    error_parts = lax.all_to_all(
        error_slots.reshape(groups * owners, capacity, local), ("dp", "latent"), split_axis=0, concat_axis=0, tiled=True
    )
    gradient = jnp.einsum("nsi,nsd->id", copies, error_parts, preferred_element_type=F32) * loss_scale
    return rebuilt_wide.astype(BF16), gradient.astype(BF16)


def solution(mesh):
    placed = (
        P(("dp", "latent"), None),
        P(("dp", "latent"), None),
        P(("dp", "latent"), None, None),
        P(("dp", "latent"), None, None),
        P("latent", "dp"),
        P(),
    )

    def body(activations, owner_ids, block_mask, latent_codes, w_dec, b_dec):
        owners = mesh.shape["latent"]
        share = owner_ids.size // owners
        fits = share % 16 == 0 and owners * SPARE % 16 == 0 and w_dec.shape[1] % (128 * STACK) == 0
        fits = fits and owners == 8 and mesh.shape["dp"] == 4
        pick = on_device if fits else on_device_wide
        return pick(activations, owner_ids, block_mask, latent_codes, w_dec, b_dec)

    return jax.shard_map(
        body,
        mesh=mesh,
        in_specs=placed,
        out_specs=(P(("dp", "latent"), None), P("latent", "dp")),
        check_vma=False,
    )
```

```python
import functools

import jax
import jax.numpy as jnp
from jax import lax
from jax.experimental import pallas as pl
from jax.experimental.pallas import tpu as pltpu
from jax.sharding import PartitionSpec as P

loss_scale = 1.0 / 32.0
SPARE = 2
STACK = 8
SENDS = (
    ["T00", "T01", "C20", "T02", "C21", "T03", "C22", "T10", "C23", "T11", "T12", "T20", "T13", "C30", "T21", "C31"]
    + ["T22", "C32", "E00", "C33", "T23", "E01", "T30", "T31", "E02", "T32", "E03", "T33", "E20", "E10", "E21", "E22"]
    + ["E11", "E23", "E12", "E30", "E31", "E13", "E32", "E33"]
)
WINDOW = 5
PIECES = 4
F32 = jnp.float32
BF16 = jnp.bfloat16


def mm(a, b):
    return jnp.dot(a, b, preferred_element_type=F32)


def swap_matrix(outer, inner):
    size = outer * inner * SPARE
    to = lax.broadcasted_iota(jnp.int32, (size, size), 0)
    at = lax.broadcasted_iota(jnp.int32, (size, size), 1)
    to_inner, to_outer = to // (outer * SPARE), to % (outer * SPARE) // SPARE
    at_outer, at_inner = at // (inner * SPARE), at % (inner * SPARE) // SPARE
    same = (to_inner == at_inner) & (to_outer == at_outer) & (to % SPARE == at % SPARE)
    return same.astype(F32).astype(BF16)


def pack_kernel(order, visits, at_ref, small_ref, codes_ref, *outs):
    messages, (pick_ref, pick_spare_ref, place_ref, place_spare_ref) = outs[:-4], outs[-4:]
    owners = len(messages)
    rows, width = codes_ref.shape[0], codes_ref.shape[1] // visits
    blocks = small_ref.shape[0] // visits - 1
    block = width // blocks
    main = rows * visits // owners
    slots = owners * (main + SPARE)
    apart = small_ref[:visits, :] ^ at_ref[0]
    relative = sum(jnp.where(apart == k, p, 0) for p, k in enumerate(order))
    eye = lax.broadcasted_iota(jnp.int32, (rows, rows), 0) == lax.broadcasted_iota(jnp.int32, (rows, rows), 1)
    lanes = [relative[g : g + 1, :] for g in range(visits)]
    columns = [jnp.sum(jnp.where(eye, lane, 0), axis=1, keepdims=True) for lane in lanes]
    column, lane = jnp.concatenate(columns, axis=0), jnp.concatenate(lanes, axis=1)
    total = rows * visits
    down = lax.broadcasted_iota(jnp.int32, (total, total), 0)
    across = lax.broadcasted_iota(jnp.int32, (total, total), 1)
    same = column == lane

    def slot_of(owner, place):
        return jnp.where(place < main, owner * main + place, owners * main + owner * SPARE + place - main)

    slot_lane = slot_of(lane, jnp.sum(jnp.where(same & (down < across), 1, 0), axis=0, keepdims=True))
    slot_column = slot_of(column, jnp.sum(jnp.where(same & (across < down), 1, 0), axis=1, keepdims=True))
    place = (lax.broadcasted_iota(jnp.int32, (slots, total), 0) == slot_lane).astype(F32)
    pick = (lax.broadcasted_iota(jnp.int32, (total, slots), 1) == slot_column).astype(F32)
    place_rows = sum(place[:, g * rows : (g + 1) * rows] for g in range(visits)).astype(BF16)
    pick_rows = sum(pick[g * rows : (g + 1) * rows, :] for g in range(visits)).astype(BF16)
    pick_ref[...] = pick_rows[:, : owners * main]
    pick_spare_ref[...] = pick_rows[:, owners * main :]
    place_ref[...] = place_rows[: owners * main, :]
    place_spare_ref[...] = place_rows[owners * main :, :]
    live = small_ref[...].astype(F32).T.astype(BF16)[:, visits:]
    used = jnp.concatenate(
        [
            jnp.concatenate(
                [
                    codes_ref[:, g * width + b * block : g * width + (b + 1) * block] * live[:, g * blocks + b : g * blocks + b + 1]
                    for b in range(blocks)
                ],
                axis=1,
            )
            for g in range(visits)
        ],
        axis=0,
    )
    sorted_codes = mm(place.astype(BF16), used).astype(BF16)
    part = width // STACK
    for q in range(STACK):
        stack(messages, q, main, sorted_codes[: owners * main, q * part : (q + 1) * part])
    spare = [sorted_codes[owners * main :, q * part : (q + 1) * part] for q in range(STACK)]
    stack_spare(messages, main, jnp.concatenate(spare, axis=0))


def stack(messages, q, main, block):
    for p, message in enumerate(messages):
        message[q * main : (q + 1) * main, :] = block[p * main : (p + 1) * main, :]


def stack_spare(messages, main, spare):
    spare = mm(swap_matrix(STACK, len(messages)), spare).astype(BF16)
    for p, message in enumerate(messages):
        message[STACK * main :, :] = spare[p * STACK * SPARE : (p + 1) * STACK * SPARE, :]


def unstacked(messages, q, main):
    return jnp.concatenate([message[q * main : (q + 1) * main, :] for message in messages], axis=0)


def unstacked_spare(messages, main):
    spare = jnp.concatenate([message[STACK * main :, :] for message in messages], axis=0)
    return mm(swap_matrix(len(messages), STACK), spare).astype(BF16)


def main_of(message):
    return message.shape[0] // STACK - SPARE


def cut(codes, pieces):
    wide = codes.shape[1] // len(pieces)
    for i, piece in enumerate(pieces):
        piece[...] = codes[:, i * wide : (i + 1) * wide]


def joined(pieces):
    return jnp.concatenate([piece[...] for piece in pieces], axis=1)


def unpack_kernel(owners, *refs):
    messages, out_ref, pieces = refs[:owners], refs[-1 - PIECES], refs[-PIECES:]
    main, part = main_of(messages[0]), messages[0].shape[1]
    spares = owners * SPARE
    spare = unstacked_spare(messages, main)
    for q in range(STACK):
        out_ref[: owners * main, q * part : (q + 1) * part] = unstacked(messages, q, main)
        out_ref[owners * main :, q * part : (q + 1) * part] = spare[q * spares : (q + 1) * spares, :]
    cut(out_ref[...], pieces)


def decode_kernel(owners, given, w_ref, *refs):
    codes = joined(refs[:given])
    messages, copies = refs[given : given + owners], refs[given + owners :]
    if copies:
        cut(codes, copies)
    main, part = main_of(messages[0]), messages[0].shape[1]
    spares = []
    for q in range(STACK):
        term = mm(codes, w_ref[:, q * part : (q + 1) * part]).astype(BF16)
        stack(messages, q, main, term[: owners * main, :])
        spares.append(term[owners * main :, :])
    stack_spare(messages, main, jnp.concatenate(spares, axis=0))


def touch_kernel(*refs):
    refs[-1][...] = jnp.zeros_like(refs[-1])


def combine_kernel(owners, place_in_ref, pick_ref, pick_spare_ref, place_ref, place_spare_ref, b_ref, act_ref, *rest):
    terms, rebuilt_ref, messages = rest[:owners], rest[-owners - 1], rest[-owners:]
    main, part = main_of(messages[0]), messages[0].shape[1]
    spares = owners * SPARE
    spare_in = unstacked_spare(terms, main)
    spare_out = []
    for q in range(STACK):
        columns = slice(q * part, (q + 1) * part)
        total = mm(pick_ref[...], unstacked(terms, q, main))
        total += mm(pick_spare_ref[...], spare_in[q * spares : (q + 1) * spares, :])
        wide = b_ref[:, columns] + total
        rebuilt_ref[:, columns] = wide.astype(BF16)
        errors = (wide - act_ref[:, columns].astype(F32)).astype(BF16)
        stack(messages, q, main, mm(place_ref[...], errors).astype(BF16))
        spare_out.append(mm(place_spare_ref[...], errors).astype(BF16))
    stack_spare(messages, main, jnp.concatenate(spare_out, axis=0))


def turn_kernel(counts, owners, main, scale, picked, *refs):
    codes, out_ref = [], refs[-1]
    for j in range(len(counts)):
        codes.append(joined(refs[sum(counts[:j]) : sum(counts[: j + 1])]).astype(F32) * scale)
    at = 0
    for code, (_, first, count) in zip(codes, picked):
        out_ref[:, at : at + count * main] = code[first * main : (first + count) * main, :].T.astype(BF16)
        at += count * main
    base = owners * main
    spare = [code[base + f * SPARE : base + (f + n) * SPARE, :] for code, (_, f, n) in zip(codes, picked)]
    out_ref[:, at:] = jnp.concatenate(spare, axis=0).T.astype(BF16)


def gradient_kernel(counts, last, codes_ref, *refs):
    own = [refs[sum(counts[:i]) : sum(counts[: i + 1])] for i in range(len(counts))]
    refs = refs[sum(counts) :]
    main, part = main_of(own[0][0]), own[0][0].shape[1]
    if last:
        base_ref, out_ref, *spare_refs, block_ref, sems = refs
    else:
        out_ref, *spare_refs = refs[-1 - len(counts) :]
    for messages, spare_ref in zip(own, spare_refs):
        spare_ref[...] = unstacked_spare(messages, main).astype(F32)

    def columns_of(q):
        return pl.ds(pl.multiple_of(q * part, part), part)

    def copy_of(q):
        return pltpu.make_async_copy(block_ref.at[:, columns_of(q)], out_ref.at[:, columns_of(q)], sems.at[q])

    def block(q, _):
        at = pl.ds(pl.multiple_of(q * main, main), main)
        arrived = [m[at, :] for messages in own for m in messages]
        spare = [
            ref[pl.ds(pl.multiple_of(q * n * SPARE, n * SPARE), n * SPARE), :] for n, ref in zip(counts, spare_refs)
        ]
        total = mm(codes_ref[...], jnp.concatenate(arrived + [jnp.concatenate(spare, axis=0).astype(BF16)], axis=0))
        if last:
            block_ref[:, columns_of(q)] = (total + base_ref[:, columns_of(q)]).astype(BF16)
            copy_of(q).start()
        else:
            out_ref[:, columns_of(q)] = total
        return _

    lax.fori_loop(0, STACK, block, 0, unroll=True)
    if last:
        for q in range(STACK):
            copy_of(q).wait()


def gate_kernel(*_):
    pass


ANYWHERE = pl.BlockSpec(memory_space=pl.ANY)


def whole(shape):
    return pl.BlockSpec(shape, lambda *_: (0,) * len(shape))


def params(mib):
    return pltpu.CompilerParams(vmem_limit_bytes=mib * 2**20)


def cost(flops, moved):
    return pl.CostEstimate(flops=int(flops), bytes_accessed=int(moved), transcendentals=0)


def on_device(activations, owner_ids, block_mask, latent_codes, w_dec, b_dec):
    rows, visits = owner_ids.shape
    width = latent_codes.shape[2]
    model = activations.shape[1]
    owners, groups = lax.axis_size("latent"), lax.axis_size("dp")
    main = rows * visits // owners
    slots = owners * (main + SPARE)
    depth = STACK * (main + SPARE)
    local = w_dec.shape[1]
    part = local // STACK
    position = jnp.stack([lax.axis_index("latent"), lax.axis_index("dp")])
    order = [4, 1, 5, 2, 6, 3, 7, 0]

    def move(x, j, k):
        if j == 0 and k == 0:
            return x
        pairs = [(i, i ^ (j * owners + k)) for i in range(groups * owners)]
        return lax.ppermute(x, ("dp", "latent"), pairs)

    def move_all(messages, j):
        return [move(message, j, k) for message, k in zip(messages, order)]

    def some(shape, dtype=BF16):
        return jax.ShapeDtypeStruct(shape, dtype)

    small = jnp.concatenate([owner_ids.T, block_mask.transpose(1, 2, 0).reshape(-1, rows)], axis=0)
    packed = pl.pallas_call(
        functools.partial(pack_kernel, order, visits),
        grid_spec=pltpu.PrefetchScalarGridSpec(
            num_scalar_prefetch=1,
            grid=(1,),
            in_specs=[whole(small.shape), whole((rows, visits * width))],
            out_specs=[whole((depth, width // STACK))] * owners
            + [whole((rows, owners * main)), whole((rows, owners * SPARE))]
            + [whole((owners * main, rows)), whole((owners * SPARE, rows))],
        ),
        out_shape=[some((depth, width // STACK))] * owners
        + [some((rows, owners * main)), some((rows, owners * SPARE))]
        + [some((owners * main, rows)), some((owners * SPARE, rows))],
        compiler_params=params(12),
        cost_estimate=cost(2 * slots * rows * visits * width, 0),
        name="pack",
    )(position, small, latent_codes.reshape(rows, -1))
    picks = packed[owners:]
    arrived = move_all(packed[:owners], 0)
    touched = pl.pallas_call(
        touch_kernel,
        in_specs=[whole(w_dec.shape), ANYWHERE],
        out_shape=some((8, 128), F32),
        compiler_params=params(12),
        cost_estimate=cost(0, 2 * width * local),
        name="touch",
    )(w_dec, arrived[0])
    piece = (slots, width // PIECES)
    own_codes, *sent_codes = pl.pallas_call(
        functools.partial(unpack_kernel, owners),
        in_specs=[whole((depth, width // STACK))] * owners + [ANYWHERE],
        out_shape=[some((slots, width))] + [some(piece)] * PIECES,
        compiler_params=params(8),
        cost_estimate=cost(0, 4 * slots * width),
        name="unpack",
    )(*arrived, touched)
    codes = [[own_codes], [move(own_codes, 1, 0)], [None] * PIECES, [None] * PIECES]

    def decode(j):
        copied = [piece] * PIECES if j == 2 else []
        return pl.pallas_call(
            functools.partial(decode_kernel, owners, len(codes[j])),
            in_specs=[whole((width, local))] + [whole(c.shape) for c in codes[j]],
            out_specs=[whole((depth, part))] * owners + [whole(c) for c in copied],
            out_shape=[some((depth, part))] * owners + [some(c) for c in copied],
            compiler_params=params(16),
            cost_estimate=cost(2 * slots * width * local, 2 * (width * local + slots * (width + local))),
            name="decode",
        )(w_dec, *codes[j])

    def combine(j, rebuilt):
        after = [] if rebuilt is None else [rebuilt]
        outs = pl.pallas_call(
            functools.partial(combine_kernel, owners),
            grid_spec=pltpu.PrefetchScalarGridSpec(
                num_scalar_prefetch=1,
                grid=(1,),
                in_specs=[whole(p.shape) for p in picks]
                + [pl.BlockSpec((1, local), lambda _, at: (0, at[1] ^ j))]
                + [pl.BlockSpec((rows, local), lambda _, at: (0, at[1] ^ j))]
                + [whole((depth, part))] * owners
                + [ANYWHERE] * len(after),
                out_specs=[pl.BlockSpec((rows, local), lambda _, at: (0, at[1] ^ j))] + [whole((depth, part))] * owners,
            ),
            out_shape=[some((rows, model))] + [some((depth, part))] * owners,
            input_output_aliases={7 + owners: 0} if after else {},
            compiler_params=params(16),
            cost_estimate=cost(4 * slots * rows * local, 2 * local * (2 * slots + 2 * rows)),
            name="combine",
        )(position, *picks, b_dec.reshape(1, -1), activations, *terms[j], *after)
        return outs[0], outs[1:]

    def gradient(picked, base, after):
        counts = [n for _, _, n in picked]
        depths = sum(counts) * (main + SPARE)
        pieces = [c for j, _, _ in picked for c in codes[j]]
        turned = pl.pallas_call(
            functools.partial(turn_kernel, [len(codes[j]) for j, _, _ in picked], owners, main, loss_scale, picked),
            in_specs=[whole(c.shape) for c in pieces],
            out_shape=some((width, depths)),
            compiler_params=params(16),
            cost_estimate=cost(0, 4 * width * depths),
            name="turn",
        )(*pieces)
        last = base is not None
        spare = [pltpu.VMEM((STACK * n * SPARE, part), F32) for n in counts]
        buffers = [pltpu.VMEM((width, local), BF16), pltpu.SemaphoreType.DMA((STACK,))] if last else []
        return pl.pallas_call(
            functools.partial(gradient_kernel, counts, last),
            in_specs=[whole(turned.shape)]
            + [whole((depth, part))] * sum(counts)
            + [whole((width, local))] * last
            + [ANYWHERE] * len(after),
            out_specs=ANYWHERE if last else whole((width, local)),
            out_shape=some((width, local), BF16 if last else F32),
            scratch_shapes=spare + buffers,
            compiler_params=params(24),
            cost_estimate=cost(2 * depths * width * local, 4 * width * local),
            name="gradient",
        )(turned, *[m for j, f, n in picked for m in errors[j][f : f + n]], *([base] if last else []), *after)

    def gate(messages, after):
        held = pl.pallas_call(
            gate_kernel,
            in_specs=[ANYWHERE] * (len(messages) + len(after)),
            out_specs=[ANYWHERE] * len(messages),
            out_shape=[some(m.shape) for m in messages],
            input_output_aliases={i: i for i in range(len(messages))},
            compiler_params=params(1),
            cost_estimate=cost(0, 0),
            name="gate",
        )(*messages, *after)
        return list(held)

    terms, errors, leaving = [[None] * owners for _ in range(groups)], [[None] * owners for _ in range(groups)], {}
    rebuilt, arrivals, held = None, list(codes[1]), []
    for kind, j, at in SENDS:
        j, at = int(j), int(at)
        if kind == "C":
            chunk, messages = codes[j], [(sent_codes[at], 2, 0, at) if j == 2 else (leaving["T", 2][owners + at], 1, 0, at)]
        else:
            chunk = (terms if kind == "T" else errors)[j]
            if (kind, j) not in leaving:
                if kind == "T":
                    leaving[kind, j] = decode(j)
                else:
                    rebuilt, leaving[kind, j] = combine(j, rebuilt)
            messages = [(leaving[kind, j][p], j, order[p], p) for p in (2 * at, 2 * at + 1)]
        for message, across, along, place in messages:
            if across or along:
                (message,) = held = gate([message], arrivals[-WINDOW:][:1] * (len(arrivals) >= WINDOW) + held)
                message = move(message, across, along)
                arrivals.append(message)
            chunk[place] = message
    half = owners // 2
    base = gradient([(0, 0, owners), (2, 0, owners), (1, 0, owners), (3, 0, half)], None, held)
    return rebuilt, gradient([(3, half, owners - half)], base, [])


def on_device_wide(activations, owner_ids, block_mask, latent_codes, w_dec, b_dec):
    row_count, visit_count = owner_ids.shape
    block_count = block_mask.shape[2]
    slab_width = latent_codes.shape[2]
    block_width = slab_width // block_count
    model_width = activations.shape[1]
    owners = lax.axis_size("latent")
    groups = lax.axis_size("dp")
    capacity = row_count * visit_count // owners + SPARE
    live = block_mask.astype(latent_codes.dtype)[:, :, :, None]
    used = (latent_codes.reshape(row_count, visit_count, block_count, block_width) * live).reshape(-1, slab_width)
    onehot = (owner_ids[:, :, None] == lax.broadcasted_iota(jnp.int32, (1, 1, owners), 2)).astype(jnp.int32)
    per_row = jnp.sum(onehot, axis=1)
    before = jnp.cumsum(per_row, axis=0) - per_row
    position = jnp.sum(onehot * before[:, None, :], axis=2)
    target_slot = (owner_ids * capacity + position).reshape(-1)
    outgoing = jnp.zeros((owners * capacity, slab_width), latent_codes.dtype)
    outgoing = outgoing.at[target_slot].set(used).reshape(owners, capacity, slab_width)
    arrived = lax.all_to_all(outgoing, "latent", split_axis=0, concat_axis=0, tiled=True)
    copies = lax.all_gather(arrived, "dp", axis=0, tiled=True)
    decoded = mm(copies.reshape(-1, slab_width), w_dec).astype(BF16)
    local = w_dec.shape[1]
    returned = lax.all_to_all(
        decoded.reshape(groups * owners, capacity, local), ("dp", "latent"), split_axis=0, concat_axis=0, tiled=True
    )
    returned = returned.reshape(groups, owners * capacity, local)
    gathered = returned[:, target_slot].reshape(groups, row_count, visit_count, local)
    gathered = jnp.sum(gathered, axis=2, dtype=F32).transpose(1, 0, 2).reshape(row_count, model_width)
    rebuilt_wide = b_dec[None, :] + gathered
    errors = (rebuilt_wide - activations.astype(F32)).astype(BF16)
    parts = jnp.repeat(errors.reshape(row_count, groups, local).transpose(1, 0, 2), visit_count, axis=1)
    error_slots = jnp.zeros((groups, owners * capacity, local), BF16).at[:, target_slot].set(parts)
    error_parts = lax.all_to_all(
        error_slots.reshape(groups * owners, capacity, local), ("dp", "latent"), split_axis=0, concat_axis=0, tiled=True
    )
    gradient = jnp.einsum("nsi,nsd->id", copies, error_parts, preferred_element_type=F32) * loss_scale
    return rebuilt_wide.astype(BF16), gradient.astype(BF16)


def solution(mesh):
    placed = (
        P(("dp", "latent"), None),
        P(("dp", "latent"), None),
        P(("dp", "latent"), None, None),
        P(("dp", "latent"), None, None),
        P("latent", "dp"),
        P(),
    )

    def body(activations, owner_ids, block_mask, latent_codes, w_dec, b_dec):
        owners = mesh.shape["latent"]
        share = owner_ids.size // owners
        fits = share % 16 == 0 and owners * SPARE % 16 == 0 and w_dec.shape[1] % (128 * STACK) == 0
        fits = fits and owners == 8 and mesh.shape["dp"] == 4
        pick = on_device if fits else on_device_wide
        return pick(activations, owner_ids, block_mask, latent_codes, w_dec, b_dec)

    return jax.shard_map(
        body,
        mesh=mesh,
        in_specs=placed,
        out_specs=(P(("dp", "latent"), None), P("latent", "dp")),
        check_vma=False,
    )
```

```python
import functools

import jax
import jax.numpy as jnp
from jax import lax
from jax.experimental import pallas as pl
from jax.experimental.pallas import tpu as pltpu
from jax.sharding import PartitionSpec as P

loss_scale = 1.0 / 32.0
SPARE = 2
STACK = 8
SENDS = (
    ["T01", "C20", "T02", "C21", "T03", "C22", "T10", "C23", "T11", "T12", "T20", "T13", "C30", "T21", "C31"]
    + ["T22", "C32", "E00", "C33", "T23", "E01", "T30", "T31", "E02", "T32", "E03", "T33", "E20", "E10", "E21", "E22"]
    + ["E11", "E23", "E30", "E12", "E31", "E13", "E33", "E32"]
)
WINDOW = 5
PIECES = 4
F32 = jnp.float32
BF16 = jnp.bfloat16


def mm(a, b):
    return jnp.dot(a, b, preferred_element_type=F32)


def swap_matrix(outer, inner):
    size = outer * inner * SPARE
    to = lax.broadcasted_iota(jnp.int32, (size, size), 0)
    at = lax.broadcasted_iota(jnp.int32, (size, size), 1)
    to_inner, to_outer = to // (outer * SPARE), to % (outer * SPARE) // SPARE
    at_outer, at_inner = at // (inner * SPARE), at % (inner * SPARE) // SPARE
    same = (to_inner == at_inner) & (to_outer == at_outer) & (to % SPARE == at % SPARE)
    return same.astype(F32).astype(BF16)


def pack_kernel(order, visits, at_ref, small_ref, codes_ref, *outs):
    messages, (pick_ref, pick_spare_ref, place_ref, place_spare_ref) = outs[:-4], outs[-4:]
    owners = len(messages)
    rows, width = codes_ref.shape[0], codes_ref.shape[1] // visits
    blocks = small_ref.shape[0] // visits - 1
    block = width // blocks
    main = rows * visits // owners
    slots = owners * (main + SPARE)
    apart = small_ref[:visits, :] ^ at_ref[0]
    relative = sum(jnp.where(apart == k, p, 0) for p, k in enumerate(order))
    eye = lax.broadcasted_iota(jnp.int32, (rows, rows), 0) == lax.broadcasted_iota(jnp.int32, (rows, rows), 1)
    lanes = [relative[g : g + 1, :] for g in range(visits)]
    columns = [jnp.sum(jnp.where(eye, lane, 0), axis=1, keepdims=True) for lane in lanes]
    column, lane = jnp.concatenate(columns, axis=0), jnp.concatenate(lanes, axis=1)
    total = rows * visits
    down = lax.broadcasted_iota(jnp.int32, (total, total), 0)
    across = lax.broadcasted_iota(jnp.int32, (total, total), 1)
    same = column == lane

    def slot_of(owner, place):
        return jnp.where(place < main, owner * main + place, owners * main + owner * SPARE + place - main)

    slot_lane = slot_of(lane, jnp.sum(jnp.where(same & (down < across), 1, 0), axis=0, keepdims=True))
    slot_column = slot_of(column, jnp.sum(jnp.where(same & (across < down), 1, 0), axis=1, keepdims=True))
    place = (lax.broadcasted_iota(jnp.int32, (slots, total), 0) == slot_lane).astype(F32)
    pick = (lax.broadcasted_iota(jnp.int32, (total, slots), 1) == slot_column).astype(F32)
    place_rows = sum(place[:, g * rows : (g + 1) * rows] for g in range(visits)).astype(BF16)
    pick_rows = sum(pick[g * rows : (g + 1) * rows, :] for g in range(visits)).astype(BF16)
    pick_ref[...] = pick_rows[:, : owners * main]
    pick_spare_ref[...] = pick_rows[:, owners * main :]
    place_ref[...] = place_rows[: owners * main, :]
    place_spare_ref[...] = place_rows[owners * main :, :]
    live = small_ref[...].astype(F32).T.astype(BF16)[:, visits:]
    used = jnp.concatenate(
        [
            jnp.concatenate(
                [
                    codes_ref[:, g * width + b * block : g * width + (b + 1) * block] * live[:, g * blocks + b : g * blocks + b + 1]
                    for b in range(blocks)
                ],
                axis=1,
            )
            for g in range(visits)
        ],
        axis=0,
    )
    sorted_codes = mm(place.astype(BF16), used).astype(BF16)
    part = width // STACK
    for q in range(STACK):
        stack(messages, q, main, sorted_codes[: owners * main, q * part : (q + 1) * part])
    spare = [sorted_codes[owners * main :, q * part : (q + 1) * part] for q in range(STACK)]
    stack_spare(messages, main, jnp.concatenate(spare, axis=0))


def stack(messages, q, main, block):
    for p, message in enumerate(messages):
        message[q * main : (q + 1) * main, :] = block[p * main : (p + 1) * main, :]


def stack_spare(messages, main, spare):
    spare = mm(swap_matrix(STACK, len(messages)), spare).astype(BF16)
    for p, message in enumerate(messages):
        message[STACK * main :, :] = spare[p * STACK * SPARE : (p + 1) * STACK * SPARE, :]


def unstacked(messages, q, main):
    return jnp.concatenate([message[q * main : (q + 1) * main, :] for message in messages], axis=0)


def unstacked_spare(messages, main):
    spare = jnp.concatenate([message[STACK * main :, :] for message in messages], axis=0)
    return mm(swap_matrix(len(messages), STACK), spare).astype(BF16)


def main_of(message):
    return message.shape[0] // STACK - SPARE


def cut(codes, pieces):
    wide = codes.shape[1] // len(pieces)
    for i, piece in enumerate(pieces):
        piece[...] = codes[:, i * wide : (i + 1) * wide]


def joined(pieces):
    return jnp.concatenate([piece[...] for piece in pieces], axis=1)


def unpack_kernel(owners, *refs):
    messages, out_ref, pieces = refs[:owners], refs[-1 - PIECES], refs[-PIECES:]
    main, part = main_of(messages[0]), messages[0].shape[1]
    spares = owners * SPARE
    spare = unstacked_spare(messages, main)
    for q in range(STACK):
        out_ref[: owners * main, q * part : (q + 1) * part] = unstacked(messages, q, main)
        out_ref[owners * main :, q * part : (q + 1) * part] = spare[q * spares : (q + 1) * spares, :]
    cut(out_ref[...], pieces)


def decode_kernel(owners, given, w_ref, *refs):
    codes = joined(refs[:given])
    messages, copies = refs[given : given + owners], refs[given + owners :]
    if copies:
        cut(codes, copies)
    main, part = main_of(messages[0]), messages[0].shape[1]
    spares = []
    for q in range(STACK):
        term = mm(codes, w_ref[:, q * part : (q + 1) * part]).astype(BF16)
        stack(messages, q, main, term[: owners * main, :])
        spares.append(term[owners * main :, :])
    stack_spare(messages, main, jnp.concatenate(spares, axis=0))


def half_decode_kernel(count, w_ref, *refs):
    given, messages = refs[:count], refs[-count:]
    main, part = main_of(given[0]), messages[0].shape[1]
    spares = count * SPARE
    lone = unstacked_spare(given, main).astype(F32)
    lone = jnp.concatenate([lone[q * spares : (q + 1) * spares, :] for q in range(STACK)], axis=1)
    lone = jnp.concatenate([lone, jnp.zeros((-spares % 16, lone.shape[1]), F32)], axis=0).astype(BF16)
    codes = jnp.concatenate([unstacked(given, q, main) for q in range(STACK)], axis=1)
    codes = jnp.concatenate([codes, lone], axis=0)
    out = []
    for q in range(STACK):
        term = mm(codes, w_ref[:, q * part : (q + 1) * part])
        stack(messages, q, main, term[: count * main, :].astype(BF16))
        out.append(term[count * main : count * main + spares, :])
    stack_spare(messages, main, jnp.concatenate(out, axis=0).astype(BF16))


def combine_kernel(owners, place_in_ref, pick_ref, pick_spare_ref, place_ref, place_spare_ref, b_ref, act_ref, *rest):
    terms, rebuilt_ref, messages = rest[:owners], rest[-owners - 1], rest[-owners:]
    main, part = main_of(messages[0]), messages[0].shape[1]
    spares = owners * SPARE
    spare_in = unstacked_spare(terms, main)
    spare_out = []
    for q in range(STACK):
        columns = slice(q * part, (q + 1) * part)
        total = mm(pick_ref[...], unstacked(terms, q, main))
        total += mm(pick_spare_ref[...], spare_in[q * spares : (q + 1) * spares, :])
        wide = b_ref[:, columns] + total
        rebuilt_ref[:, columns] = wide.astype(BF16)
        errors = (wide - act_ref[:, columns].astype(F32)).astype(BF16)
        stack(messages, q, main, mm(place_ref[...], errors).astype(BF16))
        spare_out.append(mm(place_spare_ref[...], errors).astype(BF16))
    stack_spare(messages, main, jnp.concatenate(spare_out, axis=0))


def turn_kernel(counts, owners, main, scale, picked, *refs):
    codes, out_ref = [], refs[-1]
    for j in range(len(counts)):
        codes.append(joined(refs[sum(counts[:j]) : sum(counts[: j + 1])]).astype(F32) * scale)
    at = 0
    for code, (_, first, count) in zip(codes, picked):
        out_ref[:, at : at + count * main] = code[first * main : (first + count) * main, :].T.astype(BF16)
        at += count * main
    base = owners * main
    spare = [code[base + f * SPARE : base + (f + n) * SPARE, :] for code, (_, f, n) in zip(codes, picked)]
    out_ref[:, at:] = jnp.concatenate(spare, axis=0).T.astype(BF16)


def gradient_kernel(counts, last, codes_ref, *refs):
    own = [refs[sum(counts[:i]) : sum(counts[: i + 1])] for i in range(len(counts))]
    refs = refs[sum(counts) :]
    main, part = main_of(own[0][0]), own[0][0].shape[1]
    if last:
        base_ref, out_ref, *spare_refs, block_ref, sems = refs
    else:
        out_ref, *spare_refs = refs[-1 - len(counts) :]
    for messages, spare_ref in zip(own, spare_refs):
        spare_ref[...] = unstacked_spare(messages, main).astype(F32)

    def columns_of(q):
        return pl.ds(pl.multiple_of(q * part, part), part)

    def copy_of(q):
        return pltpu.make_async_copy(block_ref.at[:, columns_of(q)], out_ref.at[:, columns_of(q)], sems.at[q])

    def block(q, _):
        at = pl.ds(pl.multiple_of(q * main, main), main)
        arrived = [m[at, :] for messages in own for m in messages]
        spare = [
            ref[pl.ds(pl.multiple_of(q * n * SPARE, n * SPARE), n * SPARE), :] for n, ref in zip(counts, spare_refs)
        ]
        total = mm(codes_ref[...], jnp.concatenate(arrived + [jnp.concatenate(spare, axis=0).astype(BF16)], axis=0))
        if last:
            block_ref[:, columns_of(q)] = (total + base_ref[:, columns_of(q)]).astype(BF16)
            copy_of(q).start()
        else:
            out_ref[:, columns_of(q)] = total
        return _

    lax.fori_loop(0, STACK, block, 0, unroll=True)
    if last:
        for q in range(STACK):
            copy_of(q).wait()


def gate_kernel(*_):
    pass


ANYWHERE = pl.BlockSpec(memory_space=pl.ANY)


def whole(shape):
    return pl.BlockSpec(shape, lambda *_: (0,) * len(shape))


def params(mib):
    return pltpu.CompilerParams(vmem_limit_bytes=mib * 2**20)


def cost(flops, moved):
    return pl.CostEstimate(flops=int(flops), bytes_accessed=int(moved), transcendentals=0)


def on_device(activations, owner_ids, block_mask, latent_codes, w_dec, b_dec):
    rows, visits = owner_ids.shape
    width = latent_codes.shape[2]
    model = activations.shape[1]
    owners, groups = lax.axis_size("latent"), lax.axis_size("dp")
    main = rows * visits // owners
    slots = owners * (main + SPARE)
    depth = STACK * (main + SPARE)
    local = w_dec.shape[1]
    part = local // STACK
    position = jnp.stack([lax.axis_index("latent"), lax.axis_index("dp")])
    order = [4, 1, 5, 2, 6, 3, 7, 0]

    def move(x, j, k):
        if j == 0 and k == 0:
            return x
        pairs = [(i, i ^ (j * owners + k)) for i in range(groups * owners)]
        return lax.ppermute(x, ("dp", "latent"), pairs)

    def move_all(messages, j):
        return [move(message, j, k) for message, k in zip(messages, order)]

    def some(shape, dtype=BF16):
        return jax.ShapeDtypeStruct(shape, dtype)

    small = jnp.concatenate([owner_ids.T, block_mask.transpose(1, 2, 0).reshape(-1, rows)], axis=0)
    packed = pl.pallas_call(
        functools.partial(pack_kernel, order, visits),
        grid_spec=pltpu.PrefetchScalarGridSpec(
            num_scalar_prefetch=1,
            grid=(1,),
            in_specs=[whole(small.shape), whole((rows, visits * width))],
            out_specs=[whole((depth, width // STACK))] * owners
            + [whole((rows, owners * main)), whole((rows, owners * SPARE))]
            + [whole((owners * main, rows)), whole((owners * SPARE, rows))],
        ),
        out_shape=[some((depth, width // STACK))] * owners
        + [some((rows, owners * main)), some((rows, owners * SPARE))]
        + [some((owners * main, rows)), some((owners * SPARE, rows))],
        compiler_params=params(12),
        cost_estimate=cost(2 * slots * rows * visits * width, 0),
        name="pack",
    )(position, small, latent_codes.reshape(rows, -1))
    picks = packed[owners:]
    arrived = move_all(packed[:owners], 0)
    def gate(messages, after):
        held = pl.pallas_call(
            gate_kernel,
            in_specs=[ANYWHERE] * (len(messages) + len(after)),
            out_specs=[ANYWHERE] * len(messages),
            out_shape=[some(m.shape) for m in messages],
            input_output_aliases={i: i for i in range(len(messages))},
            compiler_params=params(1),
            cost_estimate=cost(0, 0),
            name="gate",
        )(*messages, *after)
        return list(held)

    def half_decode(first, after):
        count = owners // 2
        return pl.pallas_call(
            functools.partial(half_decode_kernel, count),
            in_specs=[whole((width, local))]
            + [whole((depth, width // STACK))] * count
            + [ANYWHERE] * len(after),
            out_specs=[whole((depth, part))] * count,
            out_shape=[some((depth, part))] * count,
            compiler_params=params(16),
            cost_estimate=cost(slots * width * local, 2 * width * local),
            name="half_decode",
        )(w_dec, *arrived[first : first + count], *after)

    leaving, held = {("T", 0): list(half_decode(0, []))}, []
    terms, errors = [[None] * owners for _ in range(groups)], [[None] * owners for _ in range(groups)]
    for p in (0, 1):
        held = gate([leaving["T", 0][p]], held)
        terms[0][p] = move(held[0], 0, order[p])
    piece = (slots, width // PIECES)
    own_codes, *sent_codes = pl.pallas_call(
        functools.partial(unpack_kernel, owners),
        in_specs=[whole((depth, width // STACK))] * owners + [ANYWHERE],
        out_shape=[some((slots, width))] + [some(piece)] * PIECES,
        compiler_params=params(8),
        cost_estimate=cost(0, 4 * slots * width),
        name="unpack",
    )(*arrived, held[0])
    codes = [[own_codes], [move(own_codes, 1, 0)], [None] * PIECES, [None] * PIECES]
    leaving["T", 0] += half_decode(owners // 2, [held[0]])

    def decode(j):
        copied = [piece] * PIECES if j == 2 else []
        return pl.pallas_call(
            functools.partial(decode_kernel, owners, len(codes[j])),
            in_specs=[whole((width, local))] + [whole(c.shape) for c in codes[j]],
            out_specs=[whole((depth, part))] * owners + [whole(c) for c in copied],
            out_shape=[some((depth, part))] * owners + [some(c) for c in copied],
            compiler_params=params(16),
            cost_estimate=cost(2 * slots * width * local, 2 * (width * local + slots * (width + local))),
            name="decode",
        )(w_dec, *codes[j])

    def combine(j, rebuilt):
        after = [] if rebuilt is None else [rebuilt]
        outs = pl.pallas_call(
            functools.partial(combine_kernel, owners),
            grid_spec=pltpu.PrefetchScalarGridSpec(
                num_scalar_prefetch=1,
                grid=(1,),
                in_specs=[whole(p.shape) for p in picks]
                + [pl.BlockSpec((1, local), lambda _, at: (0, at[1] ^ j))]
                + [pl.BlockSpec((rows, local), lambda _, at: (0, at[1] ^ j))]
                + [whole((depth, part))] * owners
                + [ANYWHERE] * len(after),
                out_specs=[pl.BlockSpec((rows, local), lambda _, at: (0, at[1] ^ j))] + [whole((depth, part))] * owners,
            ),
            out_shape=[some((rows, model))] + [some((depth, part))] * owners,
            input_output_aliases={7 + owners: 0} if after else {},
            compiler_params=params(16),
            cost_estimate=cost(4 * slots * rows * local, 2 * local * (2 * slots + 2 * rows)),
            name="combine",
        )(position, *picks, b_dec.reshape(1, -1), activations, *terms[j], *after)
        return outs[0], outs[1:]

    def gradient(picked, base, after):
        counts = [n for _, _, n in picked]
        depths = sum(counts) * (main + SPARE)
        pieces = [c for j, _, _ in picked for c in codes[j]]
        turned = pl.pallas_call(
            functools.partial(turn_kernel, [len(codes[j]) for j, _, _ in picked], owners, main, loss_scale, picked),
            in_specs=[whole(c.shape) for c in pieces],
            out_shape=some((width, depths)),
            compiler_params=params(16),
            cost_estimate=cost(0, 4 * width * depths),
            name="turn",
        )(*pieces)
        last = base is not None
        spare = [pltpu.VMEM((STACK * n * SPARE, part), F32) for n in counts]
        buffers = [pltpu.VMEM((width, local), BF16), pltpu.SemaphoreType.DMA((STACK,))] if last else []
        return pl.pallas_call(
            functools.partial(gradient_kernel, counts, last),
            in_specs=[whole(turned.shape)]
            + [whole((depth, part))] * sum(counts)
            + [whole((width, local))] * last
            + [ANYWHERE] * len(after),
            out_specs=ANYWHERE if last else whole((width, local)),
            out_shape=some((width, local), BF16 if last else F32),
            scratch_shapes=spare + buffers,
            compiler_params=params(24),
            cost_estimate=cost(2 * depths * width * local, 4 * width * local),
            name="gradient",
        )(turned, *[m for j, f, n in picked for m in errors[j][f : f + n]], *([base] if last else []), *after)

    rebuilt, arrivals = None, codes[1] + terms[0][:2]
    for kind, j, at in SENDS:
        j, at = int(j), int(at)
        if kind == "C":
            chunk, messages = codes[j], [(sent_codes[at], 2, 0, at) if j == 2 else (leaving["T", 2][owners + at], 1, 0, at)]
        else:
            chunk = (terms if kind == "T" else errors)[j]
            if (kind, j) not in leaving:
                if kind == "T":
                    leaving[kind, j] = decode(j)
                else:
                    rebuilt, leaving[kind, j] = combine(j, rebuilt)
            messages = [(leaving[kind, j][p], j, order[p], p) for p in (2 * at, 2 * at + 1)]
        for message, across, along, place in messages:
            if across or along:
                (message,) = held = gate([message], arrivals[-WINDOW:][:1] * (len(arrivals) >= WINDOW) + held)
                message = move(message, across, along)
                arrivals.append(message)
            chunk[place] = message
    half = owners // 2
    base = gradient([(0, 0, owners), (2, 0, owners), (1, 0, owners), (3, 0, half)], None, held)
    return rebuilt, gradient([(3, half, owners - half)], base, [])


def on_device_wide(activations, owner_ids, block_mask, latent_codes, w_dec, b_dec):
    row_count, visit_count = owner_ids.shape
    block_count = block_mask.shape[2]
    slab_width = latent_codes.shape[2]
    block_width = slab_width // block_count
    model_width = activations.shape[1]
    owners = lax.axis_size("latent")
    groups = lax.axis_size("dp")
    capacity = row_count * visit_count // owners + SPARE
    live = block_mask.astype(latent_codes.dtype)[:, :, :, None]
    used = (latent_codes.reshape(row_count, visit_count, block_count, block_width) * live).reshape(-1, slab_width)
    onehot = (owner_ids[:, :, None] == lax.broadcasted_iota(jnp.int32, (1, 1, owners), 2)).astype(jnp.int32)
    per_row = jnp.sum(onehot, axis=1)
    before = jnp.cumsum(per_row, axis=0) - per_row
    position = jnp.sum(onehot * before[:, None, :], axis=2)
    target_slot = (owner_ids * capacity + position).reshape(-1)
    outgoing = jnp.zeros((owners * capacity, slab_width), latent_codes.dtype)
    outgoing = outgoing.at[target_slot].set(used).reshape(owners, capacity, slab_width)
    arrived = lax.all_to_all(outgoing, "latent", split_axis=0, concat_axis=0, tiled=True)
    copies = lax.all_gather(arrived, "dp", axis=0, tiled=True)
    decoded = mm(copies.reshape(-1, slab_width), w_dec).astype(BF16)
    local = w_dec.shape[1]
    returned = lax.all_to_all(
        decoded.reshape(groups * owners, capacity, local), ("dp", "latent"), split_axis=0, concat_axis=0, tiled=True
    )
    returned = returned.reshape(groups, owners * capacity, local)
    gathered = returned[:, target_slot].reshape(groups, row_count, visit_count, local)
    gathered = jnp.sum(gathered, axis=2, dtype=F32).transpose(1, 0, 2).reshape(row_count, model_width)
    rebuilt_wide = b_dec[None, :] + gathered
    errors = (rebuilt_wide - activations.astype(F32)).astype(BF16)
    parts = jnp.repeat(errors.reshape(row_count, groups, local).transpose(1, 0, 2), visit_count, axis=1)
    error_slots = jnp.zeros((groups, owners * capacity, local), BF16).at[:, target_slot].set(parts)
    error_parts = lax.all_to_all(
        error_slots.reshape(groups * owners, capacity, local), ("dp", "latent"), split_axis=0, concat_axis=0, tiled=True
    )
    gradient = jnp.einsum("nsi,nsd->id", copies, error_parts, preferred_element_type=F32) * loss_scale
    return rebuilt_wide.astype(BF16), gradient.astype(BF16)


def solution(mesh):
    placed = (
        P(("dp", "latent"), None),
        P(("dp", "latent"), None),
        P(("dp", "latent"), None, None),
        P(("dp", "latent"), None, None),
        P("latent", "dp"),
        P(),
    )

    def body(activations, owner_ids, block_mask, latent_codes, w_dec, b_dec):
        owners = mesh.shape["latent"]
        share = owner_ids.size // owners
        fits = share % 16 == 0 and owners * SPARE % 16 == 0 and w_dec.shape[1] % (128 * STACK) == 0
        fits = fits and owners == 8 and mesh.shape["dp"] == 4
        pick = on_device if fits else on_device_wide
        return pick(activations, owner_ids, block_mask, latent_codes, w_dec, b_dec)

    return jax.shard_map(
        body,
        mesh=mesh,
        in_specs=placed,
        out_specs=(P(("dp", "latent"), None), P("latent", "dp")),
        check_vma=False,
    )
```

```python
import functools

import jax
import jax.numpy as jnp
from jax import lax
from jax.experimental import pallas as pl
from jax.experimental.pallas import tpu as pltpu
from jax.sharding import PartitionSpec as P

loss_scale = 1.0 / 32.0
SPARE = 2
STACK = 8
SENDS = (
    ["T01", "C20", "T02", "C21", "T03", "C22", "T10", "C23", "T11", "T12", "T20", "T13", "C30", "T21", "C31"]
    + ["T22", "C32", "E00", "C33", "T23", "E01", "T30", "T31", "E02", "T32", "E03", "T33", "E20", "E10", "E21", "E22"]
    + ["E11", "E23", "E30", "E12", "E31", "E13", "E33", "E32"]
)
WINDOW = 5
PIECES = 4
F32 = jnp.float32
BF16 = jnp.bfloat16


def mm(a, b):
    return jnp.dot(a, b, preferred_element_type=F32)


def swap_matrix(outer, inner):
    size = outer * inner * SPARE
    to = lax.broadcasted_iota(jnp.int32, (size, size), 0)
    at = lax.broadcasted_iota(jnp.int32, (size, size), 1)
    to_inner, to_outer = to // (outer * SPARE), to % (outer * SPARE) // SPARE
    at_outer, at_inner = at // (inner * SPARE), at % (inner * SPARE) // SPARE
    same = (to_inner == at_inner) & (to_outer == at_outer) & (to % SPARE == at % SPARE)
    return same.astype(F32).astype(BF16)


def pack_kernel(order, visits, at_ref, small_ref, codes_ref, *outs):
    owners = len(order)
    messages, sheets = outs[:owners], outs[-4:]
    rows = small_ref.shape[1]
    blocks = small_ref.shape[0] // visits - 1
    main = rows * visits // owners
    slots = owners * (main + SPARE)
    apart = small_ref[:visits, :] ^ at_ref[0]
    relative = sum(jnp.where(apart == k, p, 0) for p, k in enumerate(order))
    eye = lax.broadcasted_iota(jnp.int32, (rows, rows), 0) == lax.broadcasted_iota(jnp.int32, (rows, rows), 1)
    lanes = [relative[g : g + 1, :] for g in range(visits)]
    columns = [jnp.sum(jnp.where(eye, lane, 0), axis=1, keepdims=True) for lane in lanes]
    column, lane = jnp.concatenate(columns, axis=0), jnp.concatenate(lanes, axis=1)
    total = rows * visits
    down = lax.broadcasted_iota(jnp.int32, (total, total), 0)
    across = lax.broadcasted_iota(jnp.int32, (total, total), 1)
    same = column == lane

    def slot_of(owner, place):
        return jnp.where(place < main, owner * main + place, owners * main + owner * SPARE + place - main)

    slot_lane = slot_of(lane, jnp.sum(jnp.where(same & (down < across), 1, 0), axis=0, keepdims=True))
    slot_column = slot_of(column, jnp.sum(jnp.where(same & (across < down), 1, 0), axis=1, keepdims=True))
    place = (lax.broadcasted_iota(jnp.int32, (slots, total), 0) == slot_lane).astype(F32)
    pick = (lax.broadcasted_iota(jnp.int32, (total, slots), 1) == slot_column).astype(F32)
    if codes_ref is None:
        pick_ref, pick_spare_ref, place_ref, place_spare_ref = sheets
        place_rows = sum(place[:, g * rows : (g + 1) * rows] for g in range(visits)).astype(BF16)
        pick_rows = sum(pick[g * rows : (g + 1) * rows, :] for g in range(visits)).astype(BF16)
        pick_ref[...] = pick_rows[:, : owners * main]
        pick_spare_ref[...] = pick_rows[:, owners * main :]
        place_ref[...] = place_rows[: owners * main, :]
        place_spare_ref[...] = place_rows[owners * main :, :]
        return
    width = codes_ref.shape[1] // visits
    block = width // blocks
    live = small_ref[...].astype(F32).T.astype(BF16)[:, visits:]
    used = jnp.concatenate(
        [
            jnp.concatenate(
                [
                    codes_ref[:, g * width + b * block : g * width + (b + 1) * block] * live[:, g * blocks + b : g * blocks + b + 1]
                    for b in range(blocks)
                ],
                axis=1,
            )
            for g in range(visits)
        ],
        axis=0,
    )
    sorted_codes = mm(place.astype(BF16), used).astype(BF16)
    part = width // STACK
    for q in range(STACK):
        stack(messages, q, main, sorted_codes[: owners * main, q * part : (q + 1) * part])
    spare = [sorted_codes[owners * main :, q * part : (q + 1) * part] for q in range(STACK)]
    stack_spare(messages, main, jnp.concatenate(spare, axis=0))


def stack(messages, q, main, block):
    for p, message in enumerate(messages):
        message[q * main : (q + 1) * main, :] = block[p * main : (p + 1) * main, :]


def stack_spare(messages, main, spare):
    spare = mm(swap_matrix(STACK, len(messages)), spare).astype(BF16)
    for p, message in enumerate(messages):
        message[STACK * main :, :] = spare[p * STACK * SPARE : (p + 1) * STACK * SPARE, :]


def unstacked(messages, q, main):
    return jnp.concatenate([message[q * main : (q + 1) * main, :] for message in messages], axis=0)


def unstacked_spare(messages, main):
    spare = jnp.concatenate([message[STACK * main :, :] for message in messages], axis=0)
    return mm(swap_matrix(len(messages), STACK), spare).astype(BF16)


def main_of(message):
    return message.shape[0] // STACK - SPARE


def cut(codes, pieces):
    wide = codes.shape[1] // len(pieces)
    for i, piece in enumerate(pieces):
        piece[...] = codes[:, i * wide : (i + 1) * wide]


def joined(pieces):
    return jnp.concatenate([piece[...] for piece in pieces], axis=1)


def unpack_kernel(owners, *refs):
    messages, out_ref, pieces = refs[:owners], refs[-1 - PIECES], refs[-PIECES:]
    main, part = main_of(messages[0]), messages[0].shape[1]
    spares = owners * SPARE
    spare = unstacked_spare(messages, main)
    for q in range(STACK):
        out_ref[: owners * main, q * part : (q + 1) * part] = unstacked(messages, q, main)
        out_ref[owners * main :, q * part : (q + 1) * part] = spare[q * spares : (q + 1) * spares, :]
    cut(out_ref[...], pieces)


def decode_kernel(owners, given, w_ref, *refs):
    codes = joined(refs[:given])
    messages, copies = refs[given : given + owners], refs[given + owners :]
    if copies:
        cut(codes, copies)
    main, part = main_of(messages[0]), messages[0].shape[1]
    spares = []
    for q in range(STACK):
        term = mm(codes, w_ref[:, q * part : (q + 1) * part]).astype(BF16)
        stack(messages, q, main, term[: owners * main, :])
        spares.append(term[owners * main :, :])
    stack_spare(messages, main, jnp.concatenate(spares, axis=0))


def places_kernel(order, visits, at_ref, small_ref, _, *outs):
    pack_kernel(order, visits, at_ref, small_ref, None, *outs)


def half_decode_kernel(count, w_ref, *refs):
    given, messages = refs[:count], refs[-count:]
    main, part = main_of(given[0]), messages[0].shape[1]
    spares = count * SPARE
    lone = unstacked_spare(given, main).astype(F32)
    lone = jnp.concatenate([lone[q * spares : (q + 1) * spares, :] for q in range(STACK)], axis=1)
    lone = jnp.concatenate([lone, jnp.zeros((-spares % 16, lone.shape[1]), F32)], axis=0).astype(BF16)
    codes = jnp.concatenate([unstacked(given, q, main) for q in range(STACK)], axis=1)
    codes = jnp.concatenate([codes, lone], axis=0)
    out = []
    for q in range(STACK):
        term = mm(codes, w_ref[:, q * part : (q + 1) * part])
        stack(messages, q, main, term[: count * main, :].astype(BF16))
        out.append(term[count * main : count * main + spares, :])
    stack_spare(messages, main, jnp.concatenate(out, axis=0).astype(BF16))


def combine_kernel(owners, place_in_ref, pick_ref, pick_spare_ref, place_ref, place_spare_ref, b_ref, act_ref, *rest):
    terms, rebuilt_ref, messages = rest[:owners], rest[-owners - 1], rest[-owners:]
    main, part = main_of(messages[0]), messages[0].shape[1]
    spares = owners * SPARE
    spare_in = unstacked_spare(terms, main)
    spare_out = []
    for q in range(STACK):
        columns = slice(q * part, (q + 1) * part)
        total = mm(pick_ref[...], unstacked(terms, q, main))
        total += mm(pick_spare_ref[...], spare_in[q * spares : (q + 1) * spares, :])
        wide = b_ref[:, columns] + total
        rebuilt_ref[:, columns] = wide.astype(BF16)
        errors = (wide - act_ref[:, columns].astype(F32)).astype(BF16)
        stack(messages, q, main, mm(place_ref[...], errors).astype(BF16))
        spare_out.append(mm(place_spare_ref[...], errors).astype(BF16))
    stack_spare(messages, main, jnp.concatenate(spare_out, axis=0))


def turn_kernel(counts, owners, main, scale, picked, *refs):
    codes, out_ref = [], refs[-1]
    for j in range(len(counts)):
        codes.append(joined(refs[sum(counts[:j]) : sum(counts[: j + 1])]).astype(F32) * scale)
    at = 0
    for code, (_, first, count) in zip(codes, picked):
        out_ref[:, at : at + count * main] = code[first * main : (first + count) * main, :].T.astype(BF16)
        at += count * main
    base = owners * main
    spare = [code[base + f * SPARE : base + (f + n) * SPARE, :] for code, (_, f, n) in zip(codes, picked)]
    out_ref[:, at:] = jnp.concatenate(spare, axis=0).T.astype(BF16)


def gradient_kernel(counts, last, codes_ref, *refs):
    own = [refs[sum(counts[:i]) : sum(counts[: i + 1])] for i in range(len(counts))]
    refs = refs[sum(counts) :]
    main, part = main_of(own[0][0]), own[0][0].shape[1]
    if last:
        base_ref, out_ref, *spare_refs, block_ref, sems = refs
    else:
        out_ref, *spare_refs = refs[-1 - len(counts) :]
    for messages, spare_ref in zip(own, spare_refs):
        spare_ref[...] = unstacked_spare(messages, main).astype(F32)

    def columns_of(q):
        return pl.ds(pl.multiple_of(q * part, part), part)

    def copy_of(q):
        return pltpu.make_async_copy(block_ref.at[:, columns_of(q)], out_ref.at[:, columns_of(q)], sems.at[q])

    def block(q, _):
        at = pl.ds(pl.multiple_of(q * main, main), main)
        arrived = [m[at, :] for messages in own for m in messages]
        spare = [
            ref[pl.ds(pl.multiple_of(q * n * SPARE, n * SPARE), n * SPARE), :] for n, ref in zip(counts, spare_refs)
        ]
        total = mm(codes_ref[...], jnp.concatenate(arrived + [jnp.concatenate(spare, axis=0).astype(BF16)], axis=0))
        if last:
            block_ref[:, columns_of(q)] = (total + base_ref[:, columns_of(q)]).astype(BF16)
            copy_of(q).start()
        else:
            out_ref[:, columns_of(q)] = total
        return _

    lax.fori_loop(0, STACK, block, 0, unroll=True)
    if last:
        for q in range(STACK):
            copy_of(q).wait()


def gate_kernel(*_):
    pass


ANYWHERE = pl.BlockSpec(memory_space=pl.ANY)


def whole(shape):
    return pl.BlockSpec(shape, lambda *_: (0,) * len(shape))


def params(mib):
    return pltpu.CompilerParams(vmem_limit_bytes=mib * 2**20)


def cost(flops, moved):
    return pl.CostEstimate(flops=int(flops), bytes_accessed=int(moved), transcendentals=0)


def on_device(activations, owner_ids, block_mask, latent_codes, w_dec, b_dec):
    rows, visits = owner_ids.shape
    width = latent_codes.shape[2]
    model = activations.shape[1]
    owners, groups = lax.axis_size("latent"), lax.axis_size("dp")
    main = rows * visits // owners
    slots = owners * (main + SPARE)
    depth = STACK * (main + SPARE)
    local = w_dec.shape[1]
    part = local // STACK
    position = jnp.stack([lax.axis_index("latent"), lax.axis_index("dp")])
    order = [4, 1, 5, 2, 6, 3, 7, 0]

    def move(x, j, k):
        if j == 0 and k == 0:
            return x
        pairs = [(i, i ^ (j * owners + k)) for i in range(groups * owners)]
        return lax.ppermute(x, ("dp", "latent"), pairs)

    def move_all(messages, j):
        return [move(message, j, k) for message, k in zip(messages, order)]

    def some(shape, dtype=BF16):
        return jax.ShapeDtypeStruct(shape, dtype)

    small = jnp.concatenate([owner_ids.T, block_mask.transpose(1, 2, 0).reshape(-1, rows)], axis=0)
    packed = pl.pallas_call(
        functools.partial(pack_kernel, order, visits),
        grid_spec=pltpu.PrefetchScalarGridSpec(
            num_scalar_prefetch=1,
            grid=(1,),
            in_specs=[whole(small.shape), whole((rows, visits * width))],
            out_specs=[whole((depth, width // STACK))] * owners,
        ),
        out_shape=[some((depth, width // STACK))] * owners,
        compiler_params=params(12),
        cost_estimate=cost(2 * slots * rows * visits * width, 0),
        name="pack",
    )(position, small, latent_codes.reshape(rows, -1))
    arrived = move_all(packed, 0)
    sheets = [(rows, owners * main), (rows, owners * SPARE), (owners * main, rows), (owners * SPARE, rows)]
    picks = pl.pallas_call(
        functools.partial(places_kernel, order, visits),
        grid_spec=pltpu.PrefetchScalarGridSpec(
            num_scalar_prefetch=1,
            grid=(1,),
            in_specs=[whole(small.shape), ANYWHERE],
            out_specs=[whole(sheet) for sheet in sheets],
        ),
        out_shape=[some(sheet) for sheet in sheets],
        compiler_params=params(8),
        cost_estimate=cost(0, 4 * slots * rows),
        name="places",
    )(position, small, arrived[0])
    def gate(messages, after):
        held = pl.pallas_call(
            gate_kernel,
            in_specs=[ANYWHERE] * (len(messages) + len(after)),
            out_specs=[ANYWHERE] * len(messages),
            out_shape=[some(m.shape) for m in messages],
            input_output_aliases={i: i for i in range(len(messages))},
            compiler_params=params(1),
            cost_estimate=cost(0, 0),
            name="gate",
        )(*messages, *after)
        return list(held)

    def half_decode(first, after):
        count = owners // 2
        return pl.pallas_call(
            functools.partial(half_decode_kernel, count),
            in_specs=[whole((width, local))]
            + [whole((depth, width // STACK))] * count
            + [ANYWHERE] * len(after),
            out_specs=[whole((depth, part))] * count,
            out_shape=[some((depth, part))] * count,
            compiler_params=params(16),
            cost_estimate=cost(slots * width * local, 2 * width * local),
            name="half_decode",
        )(w_dec, *arrived[first : first + count], *after)

    leaving, held = {("T", 0): list(half_decode(0, []))}, []
    terms, errors = [[None] * owners for _ in range(groups)], [[None] * owners for _ in range(groups)]
    for p in (0, 1):
        held = gate([leaving["T", 0][p]], held)
        terms[0][p] = move(held[0], 0, order[p])
    piece = (slots, width // PIECES)
    own_codes, *sent_codes = pl.pallas_call(
        functools.partial(unpack_kernel, owners),
        in_specs=[whole((depth, width // STACK))] * owners + [ANYWHERE],
        out_shape=[some((slots, width))] + [some(piece)] * PIECES,
        compiler_params=params(8),
        cost_estimate=cost(0, 4 * slots * width),
        name="unpack",
    )(*arrived, held[0])
    codes = [[own_codes], [move(own_codes, 1, 0)], [None] * PIECES, [None] * PIECES]
    leaving["T", 0] += half_decode(owners // 2, [held[0]])

    def decode(j):
        copied = [piece] * PIECES if j == 2 else []
        return pl.pallas_call(
            functools.partial(decode_kernel, owners, len(codes[j])),
            in_specs=[whole((width, local))] + [whole(c.shape) for c in codes[j]],
            out_specs=[whole((depth, part))] * owners + [whole(c) for c in copied],
            out_shape=[some((depth, part))] * owners + [some(c) for c in copied],
            compiler_params=params(16),
            cost_estimate=cost(2 * slots * width * local, 2 * (width * local + slots * (width + local))),
            name="decode",
        )(w_dec, *codes[j])

    def combine(j, rebuilt):
        after = [] if rebuilt is None else [rebuilt]
        outs = pl.pallas_call(
            functools.partial(combine_kernel, owners),
            grid_spec=pltpu.PrefetchScalarGridSpec(
                num_scalar_prefetch=1,
                grid=(1,),
                in_specs=[whole(p.shape) for p in picks]
                + [pl.BlockSpec((1, local), lambda _, at: (0, at[1] ^ j))]
                + [pl.BlockSpec((rows, local), lambda _, at: (0, at[1] ^ j))]
                + [whole((depth, part))] * owners
                + [ANYWHERE] * len(after),
                out_specs=[pl.BlockSpec((rows, local), lambda _, at: (0, at[1] ^ j))] + [whole((depth, part))] * owners,
            ),
            out_shape=[some((rows, model))] + [some((depth, part))] * owners,
            input_output_aliases={7 + owners: 0} if after else {},
            compiler_params=params(16),
            cost_estimate=cost(4 * slots * rows * local, 2 * local * (2 * slots + 2 * rows)),
            name="combine",
        )(position, *picks, b_dec.reshape(1, -1), activations, *terms[j], *after)
        return outs[0], outs[1:]

    def gradient(picked, base, after):
        counts = [n for _, _, n in picked]
        depths = sum(counts) * (main + SPARE)
        pieces = [c for j, _, _ in picked for c in codes[j]]
        turned = pl.pallas_call(
            functools.partial(turn_kernel, [len(codes[j]) for j, _, _ in picked], owners, main, loss_scale, picked),
            in_specs=[whole(c.shape) for c in pieces],
            out_shape=some((width, depths)),
            compiler_params=params(16),
            cost_estimate=cost(0, 4 * width * depths),
            name="turn",
        )(*pieces)
        last = base is not None
        spare = [pltpu.VMEM((STACK * n * SPARE, part), F32) for n in counts]
        buffers = [pltpu.VMEM((width, local), BF16), pltpu.SemaphoreType.DMA((STACK,))] if last else []
        return pl.pallas_call(
            functools.partial(gradient_kernel, counts, last),
            in_specs=[whole(turned.shape)]
            + [whole((depth, part))] * sum(counts)
            + [whole((width, local))] * last
            + [ANYWHERE] * len(after),
            out_specs=ANYWHERE if last else whole((width, local)),
            out_shape=some((width, local), BF16 if last else F32),
            scratch_shapes=spare + buffers,
            compiler_params=params(24),
            cost_estimate=cost(2 * depths * width * local, 4 * width * local),
            name="gradient",
        )(turned, *[m for j, f, n in picked for m in errors[j][f : f + n]], *([base] if last else []), *after)

    rebuilt, arrivals = None, codes[1] + terms[0][:2]
    for kind, j, at in SENDS:
        j, at = int(j), int(at)
        if kind == "C":
            chunk, messages = codes[j], [(sent_codes[at], 2, 0, at) if j == 2 else (leaving["T", 2][owners + at], 1, 0, at)]
        else:
            chunk = (terms if kind == "T" else errors)[j]
            if (kind, j) not in leaving:
                if kind == "T":
                    leaving[kind, j] = decode(j)
                else:
                    rebuilt, leaving[kind, j] = combine(j, rebuilt)
            messages = [(leaving[kind, j][p], j, order[p], p) for p in (2 * at, 2 * at + 1)]
        for message, across, along, place in messages:
            if across or along:
                (message,) = held = gate([message], arrivals[-WINDOW:][:1] * (len(arrivals) >= WINDOW) + held)
                message = move(message, across, along)
                arrivals.append(message)
            chunk[place] = message
    half = owners // 2
    base = gradient([(0, 0, owners), (2, 0, owners), (1, 0, owners), (3, 0, half)], None, held)
    return rebuilt, gradient([(3, half, owners - half)], base, [])


def on_device_wide(activations, owner_ids, block_mask, latent_codes, w_dec, b_dec):
    row_count, visit_count = owner_ids.shape
    block_count = block_mask.shape[2]
    slab_width = latent_codes.shape[2]
    block_width = slab_width // block_count
    model_width = activations.shape[1]
    owners = lax.axis_size("latent")
    groups = lax.axis_size("dp")
    capacity = row_count * visit_count // owners + SPARE
    live = block_mask.astype(latent_codes.dtype)[:, :, :, None]
    used = (latent_codes.reshape(row_count, visit_count, block_count, block_width) * live).reshape(-1, slab_width)
    onehot = (owner_ids[:, :, None] == lax.broadcasted_iota(jnp.int32, (1, 1, owners), 2)).astype(jnp.int32)
    per_row = jnp.sum(onehot, axis=1)
    before = jnp.cumsum(per_row, axis=0) - per_row
    position = jnp.sum(onehot * before[:, None, :], axis=2)
    target_slot = (owner_ids * capacity + position).reshape(-1)
    outgoing = jnp.zeros((owners * capacity, slab_width), latent_codes.dtype)
    outgoing = outgoing.at[target_slot].set(used).reshape(owners, capacity, slab_width)
    arrived = lax.all_to_all(outgoing, "latent", split_axis=0, concat_axis=0, tiled=True)
    copies = lax.all_gather(arrived, "dp", axis=0, tiled=True)
    decoded = mm(copies.reshape(-1, slab_width), w_dec).astype(BF16)
    local = w_dec.shape[1]
    returned = lax.all_to_all(
        decoded.reshape(groups * owners, capacity, local), ("dp", "latent"), split_axis=0, concat_axis=0, tiled=True
    )
    returned = returned.reshape(groups, owners * capacity, local)
    gathered = returned[:, target_slot].reshape(groups, row_count, visit_count, local)
    gathered = jnp.sum(gathered, axis=2, dtype=F32).transpose(1, 0, 2).reshape(row_count, model_width)
    rebuilt_wide = b_dec[None, :] + gathered
    errors = (rebuilt_wide - activations.astype(F32)).astype(BF16)
    parts = jnp.repeat(errors.reshape(row_count, groups, local).transpose(1, 0, 2), visit_count, axis=1)
    error_slots = jnp.zeros((groups, owners * capacity, local), BF16).at[:, target_slot].set(parts)
    error_parts = lax.all_to_all(
        error_slots.reshape(groups * owners, capacity, local), ("dp", "latent"), split_axis=0, concat_axis=0, tiled=True
    )
    gradient = jnp.einsum("nsi,nsd->id", copies, error_parts, preferred_element_type=F32) * loss_scale
    return rebuilt_wide.astype(BF16), gradient.astype(BF16)


def solution(mesh):
    placed = (
        P(("dp", "latent"), None),
        P(("dp", "latent"), None),
        P(("dp", "latent"), None, None),
        P(("dp", "latent"), None, None),
        P("latent", "dp"),
        P(),
    )

    def body(activations, owner_ids, block_mask, latent_codes, w_dec, b_dec):
        owners = mesh.shape["latent"]
        share = owner_ids.size // owners
        fits = share % 16 == 0 and owners * SPARE % 16 == 0 and w_dec.shape[1] % (128 * STACK) == 0
        fits = fits and owners == 8 and mesh.shape["dp"] == 4
        pick = on_device if fits else on_device_wide
        return pick(activations, owner_ids, block_mask, latent_codes, w_dec, b_dec)

    return jax.shard_map(
        body,
        mesh=mesh,
        in_specs=placed,
        out_specs=(P(("dp", "latent"), None), P("latent", "dp")),
        check_vma=False,
    )
```

```python
import functools

import jax
import jax.numpy as jnp
from jax import lax
from jax.experimental import pallas as pl
from jax.experimental.pallas import tpu as pltpu
from jax.sharding import PartitionSpec as P

loss_scale = 1.0 / 32.0
SPARE = 2
STACK = 8
SENDS = (
    ["T01", "C20", "T02", "C21", "T03", "C22", "T10", "C23", "T11", "T12", "T20", "T13", "C30", "T21", "C31"]
    + ["T22", "C32", "E00", "C33", "T23", "E01", "T30", "E02", "T31", "T32", "E03", "T33", "E20", "E10", "E21", "E11"]
    + ["E22", "E23", "E30", "E12", "E31", "E13", "E33", "E32"]
)
WINDOW = 5
PIECES = 4
F32 = jnp.float32
BF16 = jnp.bfloat16


def mm(a, b):
    return jnp.dot(a, b, preferred_element_type=F32)


def swap_matrix(outer, inner):
    size = outer * inner * SPARE
    to = lax.broadcasted_iota(jnp.int32, (size, size), 0)
    at = lax.broadcasted_iota(jnp.int32, (size, size), 1)
    to_inner, to_outer = to // (outer * SPARE), to % (outer * SPARE) // SPARE
    at_outer, at_inner = at // (inner * SPARE), at % (inner * SPARE) // SPARE
    same = (to_inner == at_inner) & (to_outer == at_outer) & (to % SPARE == at % SPARE)
    return same.astype(F32).astype(BF16)


def pack_kernel(order, visits, at_ref, small_ref, codes_ref, *outs):
    owners = len(order)
    messages, sheets = outs[:owners], outs[-4:]
    rows = small_ref.shape[1]
    blocks = small_ref.shape[0] // visits - 1
    main = rows * visits // owners
    slots = owners * (main + SPARE)
    apart = small_ref[:visits, :] ^ at_ref[0]
    relative = sum(jnp.where(apart == k, p, 0) for p, k in enumerate(order))
    eye = lax.broadcasted_iota(jnp.int32, (rows, rows), 0) == lax.broadcasted_iota(jnp.int32, (rows, rows), 1)
    lanes = [relative[g : g + 1, :] for g in range(visits)]
    columns = [jnp.sum(jnp.where(eye, lane, 0), axis=1, keepdims=True) for lane in lanes]
    column, lane = jnp.concatenate(columns, axis=0), jnp.concatenate(lanes, axis=1)
    total = rows * visits
    down = lax.broadcasted_iota(jnp.int32, (total, total), 0)
    across = lax.broadcasted_iota(jnp.int32, (total, total), 1)
    same = column == lane

    def slot_of(owner, place):
        return jnp.where(place < main, owner * main + place, owners * main + owner * SPARE + place - main)

    slot_lane = slot_of(lane, jnp.sum(jnp.where(same & (down < across), 1, 0), axis=0, keepdims=True))
    slot_column = slot_of(column, jnp.sum(jnp.where(same & (across < down), 1, 0), axis=1, keepdims=True))
    place = (lax.broadcasted_iota(jnp.int32, (slots, total), 0) == slot_lane).astype(F32)
    pick = (lax.broadcasted_iota(jnp.int32, (total, slots), 1) == slot_column).astype(F32)
    if codes_ref is None:
        pick_ref, pick_spare_ref, place_ref, place_spare_ref = sheets
        place_rows = sum(place[:, g * rows : (g + 1) * rows] for g in range(visits)).astype(BF16)
        pick_rows = sum(pick[g * rows : (g + 1) * rows, :] for g in range(visits)).astype(BF16)
        pick_ref[...] = pick_rows[:, : owners * main]
        pick_spare_ref[...] = pick_rows[:, owners * main :]
        place_ref[...] = place_rows[: owners * main, :]
        place_spare_ref[...] = place_rows[owners * main :, :]
        return
    width = codes_ref.shape[1] // visits
    block = width // blocks
    live = small_ref[...].astype(F32).T.astype(BF16)[:, visits:]
    used = jnp.concatenate(
        [
            jnp.concatenate(
                [
                    codes_ref[:, g * width + b * block : g * width + (b + 1) * block] * live[:, g * blocks + b : g * blocks + b + 1]
                    for b in range(blocks)
                ],
                axis=1,
            )
            for g in range(visits)
        ],
        axis=0,
    )
    sorted_codes = mm(place.astype(BF16), used).astype(BF16)
    part = width // STACK
    for q in range(STACK):
        stack(messages, q, main, sorted_codes[: owners * main, q * part : (q + 1) * part])
    spare = [sorted_codes[owners * main :, q * part : (q + 1) * part] for q in range(STACK)]
    stack_spare(messages, main, jnp.concatenate(spare, axis=0))


def stack(messages, q, main, block):
    for p, message in enumerate(messages):
        message[q * main : (q + 1) * main, :] = block[p * main : (p + 1) * main, :]


def stack_spare(messages, main, spare):
    spare = mm(swap_matrix(STACK, len(messages)), spare).astype(BF16)
    for p, message in enumerate(messages):
        message[STACK * main :, :] = spare[p * STACK * SPARE : (p + 1) * STACK * SPARE, :]


def unstacked(messages, q, main):
    return jnp.concatenate([message[q * main : (q + 1) * main, :] for message in messages], axis=0)


def unstacked_spare(messages, main):
    spare = jnp.concatenate([message[STACK * main :, :] for message in messages], axis=0)
    return mm(swap_matrix(len(messages), STACK), spare).astype(BF16)


def main_of(message):
    return message.shape[0] // STACK - SPARE


def cut(codes, pieces):
    wide = codes.shape[1] // len(pieces)
    for i, piece in enumerate(pieces):
        piece[...] = codes[:, i * wide : (i + 1) * wide]


def joined(pieces):
    return jnp.concatenate([piece[...] for piece in pieces], axis=1)


def unpack_kernel(owners, *refs):
    messages, out_ref, pieces = refs[:owners], refs[-1 - PIECES], refs[-PIECES:]
    main, part = main_of(messages[0]), messages[0].shape[1]
    spares = owners * SPARE
    spare = unstacked_spare(messages, main)
    for q in range(STACK):
        out_ref[: owners * main, q * part : (q + 1) * part] = unstacked(messages, q, main)
        out_ref[owners * main :, q * part : (q + 1) * part] = spare[q * spares : (q + 1) * spares, :]
    cut(out_ref[...], pieces)


def decode_kernel(owners, given, w_ref, *refs):
    codes = joined(refs[:given])
    messages, copies = refs[given : given + owners], refs[given + owners :]
    if copies:
        cut(codes, copies)
    main, part = main_of(messages[0]), messages[0].shape[1]
    spares = []
    for q in range(STACK):
        term = mm(codes, w_ref[:, q * part : (q + 1) * part]).astype(BF16)
        stack(messages, q, main, term[: owners * main, :])
        spares.append(term[owners * main :, :])
    stack_spare(messages, main, jnp.concatenate(spares, axis=0))


def places_kernel(order, visits, at_ref, small_ref, _, *outs):
    pack_kernel(order, visits, at_ref, small_ref, None, *outs)


def half_decode_kernel(count, w_ref, *refs):
    given, messages = refs[:count], refs[-count:]
    main, part = main_of(given[0]), messages[0].shape[1]
    spares = count * SPARE
    lone = unstacked_spare(given, main).astype(F32)
    lone = jnp.concatenate([lone[q * spares : (q + 1) * spares, :] for q in range(STACK)], axis=1)
    lone = jnp.concatenate([lone, jnp.zeros((-spares % 16, lone.shape[1]), F32)], axis=0).astype(BF16)
    codes = jnp.concatenate([unstacked(given, q, main) for q in range(STACK)], axis=1)
    codes = jnp.concatenate([codes, lone], axis=0)
    out = []
    for q in range(STACK):
        term = mm(codes, w_ref[:, q * part : (q + 1) * part])
        stack(messages, q, main, term[: count * main, :].astype(BF16))
        out.append(term[count * main : count * main + spares, :])
    stack_spare(messages, main, jnp.concatenate(out, axis=0).astype(BF16))


def combine_kernel(owners, place_in_ref, pick_ref, pick_spare_ref, place_ref, place_spare_ref, b_ref, act_ref, *rest):
    terms, rebuilt_ref, messages = rest[:owners], rest[-owners - 1], rest[-owners:]
    main, part = main_of(messages[0]), messages[0].shape[1]
    spares = owners * SPARE
    spare_in = unstacked_spare(terms, main)
    spare_out = []
    for q in range(STACK):
        columns = slice(q * part, (q + 1) * part)
        total = mm(pick_ref[...], unstacked(terms, q, main))
        total += mm(pick_spare_ref[...], spare_in[q * spares : (q + 1) * spares, :])
        wide = b_ref[:, columns] + total
        rebuilt_ref[:, columns] = wide.astype(BF16)
        errors = (wide - act_ref[:, columns].astype(F32)).astype(BF16)
        stack(messages, q, main, mm(place_ref[...], errors).astype(BF16))
        spare_out.append(mm(place_spare_ref[...], errors).astype(BF16))
    stack_spare(messages, main, jnp.concatenate(spare_out, axis=0))


def turn_kernel(counts, owners, main, scale, picked, *refs):
    codes, out_ref = [], refs[-1]
    for j in range(len(counts)):
        codes.append(joined(refs[sum(counts[:j]) : sum(counts[: j + 1])]).astype(F32) * scale)
    at = 0
    for code, (_, first, count) in zip(codes, picked):
        out_ref[:, at : at + count * main] = code[first * main : (first + count) * main, :].T.astype(BF16)
        at += count * main
    base = owners * main
    spare = [code[base + f * SPARE : base + (f + n) * SPARE, :] for code, (_, f, n) in zip(codes, picked)]
    out_ref[:, at:] = jnp.concatenate(spare, axis=0).T.astype(BF16)


def gradient_kernel(counts, last, codes_ref, *refs):
    own = [refs[sum(counts[:i]) : sum(counts[: i + 1])] for i in range(len(counts))]
    refs = refs[sum(counts) :]
    main, part = main_of(own[0][0]), own[0][0].shape[1]
    if last:
        base_ref, out_ref, *spare_refs, block_ref, sems = refs
    else:
        out_ref, *spare_refs = refs[-1 - len(counts) :]
    for messages, spare_ref in zip(own, spare_refs):
        spare_ref[...] = unstacked_spare(messages, main).astype(F32)

    def columns_of(q):
        return pl.ds(pl.multiple_of(q * part, part), part)

    def copy_of(q):
        return pltpu.make_async_copy(block_ref.at[:, columns_of(q)], out_ref.at[:, columns_of(q)], sems.at[q])

    def block(q, _):
        at = pl.ds(pl.multiple_of(q * main, main), main)
        arrived = [m[at, :] for messages in own for m in messages]
        spare = [
            ref[pl.ds(pl.multiple_of(q * n * SPARE, n * SPARE), n * SPARE), :] for n, ref in zip(counts, spare_refs)
        ]
        total = mm(codes_ref[...], jnp.concatenate(arrived + [jnp.concatenate(spare, axis=0).astype(BF16)], axis=0))
        if last:
            block_ref[:, columns_of(q)] = (total + base_ref[:, columns_of(q)]).astype(BF16)
            copy_of(q).start()
        else:
            out_ref[:, columns_of(q)] = total
        return _

    lax.fori_loop(0, STACK, block, 0, unroll=True)
    if last:
        for q in range(STACK):
            copy_of(q).wait()


def gate_kernel(*_):
    pass


ANYWHERE = pl.BlockSpec(memory_space=pl.ANY)


def whole(shape):
    return pl.BlockSpec(shape, lambda *_: (0,) * len(shape))


def params(mib):
    return pltpu.CompilerParams(vmem_limit_bytes=mib * 2**20)


def cost(flops, moved):
    return pl.CostEstimate(flops=int(flops), bytes_accessed=int(moved), transcendentals=0)


def on_device(activations, owner_ids, block_mask, latent_codes, w_dec, b_dec):
    rows, visits = owner_ids.shape
    width = latent_codes.shape[2]
    model = activations.shape[1]
    owners, groups = lax.axis_size("latent"), lax.axis_size("dp")
    main = rows * visits // owners
    slots = owners * (main + SPARE)
    depth = STACK * (main + SPARE)
    local = w_dec.shape[1]
    part = local // STACK
    position = jnp.stack([lax.axis_index("latent"), lax.axis_index("dp")])
    order = [4, 1, 5, 2, 6, 3, 7, 0]

    def move(x, j, k):
        if j == 0 and k == 0:
            return x
        pairs = [(i, i ^ (j * owners + k)) for i in range(groups * owners)]
        return lax.ppermute(x, ("dp", "latent"), pairs)

    def move_all(messages, j):
        return [move(message, j, k) for message, k in zip(messages, order)]

    def some(shape, dtype=BF16):
        return jax.ShapeDtypeStruct(shape, dtype)

    small = jnp.concatenate([owner_ids.T, block_mask.transpose(1, 2, 0).reshape(-1, rows)], axis=0)
    packed = pl.pallas_call(
        functools.partial(pack_kernel, order, visits),
        grid_spec=pltpu.PrefetchScalarGridSpec(
            num_scalar_prefetch=1,
            grid=(1,),
            in_specs=[whole(small.shape), whole((rows, visits * width))],
            out_specs=[whole((depth, width // STACK))] * owners,
        ),
        out_shape=[some((depth, width // STACK))] * owners,
        compiler_params=params(12),
        cost_estimate=cost(2 * slots * rows * visits * width, 0),
        name="pack",
    )(position, small, latent_codes.reshape(rows, -1))
    arrived = move_all(packed, 0)
    sheets = [(rows, owners * main), (rows, owners * SPARE), (owners * main, rows), (owners * SPARE, rows)]
    picks = pl.pallas_call(
        functools.partial(places_kernel, order, visits),
        grid_spec=pltpu.PrefetchScalarGridSpec(
            num_scalar_prefetch=1,
            grid=(1,),
            in_specs=[whole(small.shape), ANYWHERE],
            out_specs=[whole(sheet) for sheet in sheets],
        ),
        out_shape=[some(sheet) for sheet in sheets],
        compiler_params=params(8),
        cost_estimate=cost(0, 4 * slots * rows),
        name="places",
    )(position, small, arrived[0])
    def gate(messages, after):
        held = pl.pallas_call(
            gate_kernel,
            in_specs=[ANYWHERE] * (len(messages) + len(after)),
            out_specs=[ANYWHERE] * len(messages),
            out_shape=[some(m.shape) for m in messages],
            input_output_aliases={i: i for i in range(len(messages))},
            compiler_params=params(1),
            cost_estimate=cost(0, 0),
            name="gate",
        )(*messages, *after)
        return list(held)

    def half_decode(first, after):
        count = owners // 2
        return pl.pallas_call(
            functools.partial(half_decode_kernel, count),
            in_specs=[whole((width, local))]
            + [whole((depth, width // STACK))] * count
            + [ANYWHERE] * len(after),
            out_specs=[whole((depth, part))] * count,
            out_shape=[some((depth, part))] * count,
            compiler_params=params(16),
            cost_estimate=cost(slots * width * local, 2 * width * local),
            name="half_decode",
        )(w_dec, *arrived[first : first + count], *after)

    leaving, held = {("T", 0): list(half_decode(0, []))}, []
    terms, errors = [[None] * owners for _ in range(groups)], [[None] * owners for _ in range(groups)]
    for p in (0, 1):
        held = gate([leaving["T", 0][p]], held)
        terms[0][p] = move(held[0], 0, order[p])
    piece = (slots, width // PIECES)
    own_codes, *sent_codes = pl.pallas_call(
        functools.partial(unpack_kernel, owners),
        in_specs=[whole((depth, width // STACK))] * owners + [ANYWHERE],
        out_shape=[some((slots, width))] + [some(piece)] * PIECES,
        compiler_params=params(8),
        cost_estimate=cost(0, 4 * slots * width),
        name="unpack",
    )(*arrived, held[0])
    codes = [[own_codes], [move(own_codes, 1, 0)], [None] * PIECES, [None] * PIECES]
    leaving["T", 0] += half_decode(owners // 2, [held[0]])

    def decode(j):
        copied = [piece] * PIECES if j == 2 else []
        return pl.pallas_call(
            functools.partial(decode_kernel, owners, len(codes[j])),
            in_specs=[whole((width, local))] + [whole(c.shape) for c in codes[j]],
            out_specs=[whole((depth, part))] * owners + [whole(c) for c in copied],
            out_shape=[some((depth, part))] * owners + [some(c) for c in copied],
            compiler_params=params(16),
            cost_estimate=cost(2 * slots * width * local, 2 * (width * local + slots * (width + local))),
            name="decode",
        )(w_dec, *codes[j])

    def combine(j, rebuilt):
        after = [] if rebuilt is None else [rebuilt]
        outs = pl.pallas_call(
            functools.partial(combine_kernel, owners),
            grid_spec=pltpu.PrefetchScalarGridSpec(
                num_scalar_prefetch=1,
                grid=(1,),
                in_specs=[whole(p.shape) for p in picks]
                + [pl.BlockSpec((1, local), lambda _, at: (0, at[1] ^ j))]
                + [pl.BlockSpec((rows, local), lambda _, at: (0, at[1] ^ j))]
                + [whole((depth, part))] * owners
                + [ANYWHERE] * len(after),
                out_specs=[pl.BlockSpec((rows, local), lambda _, at: (0, at[1] ^ j))] + [whole((depth, part))] * owners,
            ),
            out_shape=[some((rows, model))] + [some((depth, part))] * owners,
            input_output_aliases={7 + owners: 0} if after else {},
            compiler_params=params(16),
            cost_estimate=cost(4 * slots * rows * local, 2 * local * (2 * slots + 2 * rows)),
            name="combine",
        )(position, *picks, b_dec.reshape(1, -1), activations, *terms[j], *after)
        return outs[0], outs[1:]

    def gradient(picked, base, after):
        counts = [n for _, _, n in picked]
        depths = sum(counts) * (main + SPARE)
        pieces = [c for j, _, _ in picked for c in codes[j]]
        turned = pl.pallas_call(
            functools.partial(turn_kernel, [len(codes[j]) for j, _, _ in picked], owners, main, loss_scale, picked),
            in_specs=[whole(c.shape) for c in pieces],
            out_shape=some((width, depths)),
            compiler_params=params(16),
            cost_estimate=cost(0, 4 * width * depths),
            name="turn",
        )(*pieces)
        last = base is not None
        spare = [pltpu.VMEM((STACK * n * SPARE, part), F32) for n in counts]
        buffers = [pltpu.VMEM((width, local), BF16), pltpu.SemaphoreType.DMA((STACK,))] if last else []
        return pl.pallas_call(
            functools.partial(gradient_kernel, counts, last),
            in_specs=[whole(turned.shape)]
            + [whole((depth, part))] * sum(counts)
            + [whole((width, local))] * last
            + [ANYWHERE] * len(after),
            out_specs=ANYWHERE if last else whole((width, local)),
            out_shape=some((width, local), BF16 if last else F32),
            scratch_shapes=spare + buffers,
            compiler_params=params(24),
            cost_estimate=cost(2 * depths * width * local, 4 * width * local),
            name="gradient",
        )(turned, *[m for j, f, n in picked for m in errors[j][f : f + n]], *([base] if last else []), *after)

    rebuilt, arrivals = None, codes[1] + terms[0][:2]
    for kind, j, at in SENDS:
        j, at = int(j), int(at)
        if kind == "C":
            chunk, messages = codes[j], [(sent_codes[at], 2, 0, at) if j == 2 else (leaving["T", 2][owners + at], 1, 0, at)]
        else:
            chunk = (terms if kind == "T" else errors)[j]
            if (kind, j) not in leaving:
                if kind == "T":
                    leaving[kind, j] = decode(j)
                else:
                    rebuilt, leaving[kind, j] = combine(j, rebuilt)
            messages = [(leaving[kind, j][p], j, order[p], p) for p in (2 * at, 2 * at + 1)]
        for message, across, along, place in messages:
            if across or along:
                (message,) = held = gate([message], arrivals[-WINDOW:][:1] * (len(arrivals) >= WINDOW) + held)
                message = move(message, across, along)
                arrivals.append(message)
            chunk[place] = message
    half = owners // 2
    base = gradient([(0, 0, owners), (2, 0, owners), (1, 0, owners), (3, 0, half)], None, held)
    return rebuilt, gradient([(3, half, owners - half)], base, [])


def on_device_wide(activations, owner_ids, block_mask, latent_codes, w_dec, b_dec):
    row_count, visit_count = owner_ids.shape
    block_count = block_mask.shape[2]
    slab_width = latent_codes.shape[2]
    block_width = slab_width // block_count
    model_width = activations.shape[1]
    owners = lax.axis_size("latent")
    groups = lax.axis_size("dp")
    capacity = row_count * visit_count // owners + SPARE
    live = block_mask.astype(latent_codes.dtype)[:, :, :, None]
    used = (latent_codes.reshape(row_count, visit_count, block_count, block_width) * live).reshape(-1, slab_width)
    onehot = (owner_ids[:, :, None] == lax.broadcasted_iota(jnp.int32, (1, 1, owners), 2)).astype(jnp.int32)
    per_row = jnp.sum(onehot, axis=1)
    before = jnp.cumsum(per_row, axis=0) - per_row
    position = jnp.sum(onehot * before[:, None, :], axis=2)
    target_slot = (owner_ids * capacity + position).reshape(-1)
    outgoing = jnp.zeros((owners * capacity, slab_width), latent_codes.dtype)
    outgoing = outgoing.at[target_slot].set(used).reshape(owners, capacity, slab_width)
    arrived = lax.all_to_all(outgoing, "latent", split_axis=0, concat_axis=0, tiled=True)
    copies = lax.all_gather(arrived, "dp", axis=0, tiled=True)
    decoded = mm(copies.reshape(-1, slab_width), w_dec).astype(BF16)
    local = w_dec.shape[1]
    returned = lax.all_to_all(
        decoded.reshape(groups * owners, capacity, local), ("dp", "latent"), split_axis=0, concat_axis=0, tiled=True
    )
    returned = returned.reshape(groups, owners * capacity, local)
    gathered = returned[:, target_slot].reshape(groups, row_count, visit_count, local)
    gathered = jnp.sum(gathered, axis=2, dtype=F32).transpose(1, 0, 2).reshape(row_count, model_width)
    rebuilt_wide = b_dec[None, :] + gathered
    errors = (rebuilt_wide - activations.astype(F32)).astype(BF16)
    parts = jnp.repeat(errors.reshape(row_count, groups, local).transpose(1, 0, 2), visit_count, axis=1)
    error_slots = jnp.zeros((groups, owners * capacity, local), BF16).at[:, target_slot].set(parts)
    error_parts = lax.all_to_all(
        error_slots.reshape(groups * owners, capacity, local), ("dp", "latent"), split_axis=0, concat_axis=0, tiled=True
    )
    gradient = jnp.einsum("nsi,nsd->id", copies, error_parts, preferred_element_type=F32) * loss_scale
    return rebuilt_wide.astype(BF16), gradient.astype(BF16)


def solution(mesh):
    placed = (
        P(("dp", "latent"), None),
        P(("dp", "latent"), None),
        P(("dp", "latent"), None, None),
        P(("dp", "latent"), None, None),
        P("latent", "dp"),
        P(),
    )

    def body(activations, owner_ids, block_mask, latent_codes, w_dec, b_dec):
        owners = mesh.shape["latent"]
        share = owner_ids.size // owners
        fits = share % 16 == 0 and owners * SPARE % 16 == 0 and w_dec.shape[1] % (128 * STACK) == 0
        fits = fits and owners == 8 and mesh.shape["dp"] == 4
        pick = on_device if fits else on_device_wide
        return pick(activations, owner_ids, block_mask, latent_codes, w_dec, b_dec)

    return jax.shard_map(
        body,
        mesh=mesh,
        in_specs=placed,
        out_specs=(P(("dp", "latent"), None), P("latent", "dp")),
        check_vma=False,
    )
```
